32 devices in a mesh: prompt: 8 (over z, core), resp: 4 (over y, x).
Axes of the slice: x: 2, y: 2, z: 4, core: 2. Of those that a mesh axis runs over, the one named last changes fastest.
Arguments:
- answer_asking_tensor: bfloat16 [8, 4, 256, 2048], P('prompt', 'resp'), may hold values from -5 to 5
- answer_lookup_tensor: bfloat16 [8, 4, 256, 512], P('prompt', 'resp'), may hold values from -6 to 6
- answer_content_tensor: bfloat16 [8, 4, 256, 512], P('prompt', 'resp'), may hold values from -6 to 6
- unweighted_mixing_backprop: bfloat16 [8, 4, 256, 2048], P('prompt', 'resp'), may hold values from -6 to 6
- question_lookup_tensor: bfloat16 [8, 256, 512], P('prompt', 'resp'), may hold values from -6 to 6
- question_content_tensor: bfloat16 [8, 256, 512], P('prompt', 'resp'), may hold values from -6 to 6
- kept_rollout_number: int32 [8], P('prompt'), may hold values from 2 to 4, as said below
- spaces_kept_leading: int32 [8, 4], P('prompt'), may hold values from 0 to 3, each once within a row
- answer_span_tilecounts: int32 [8, 4], P('prompt', 'resp'), may hold values from 1 to 2
- rollout_payoffs: float32 [8, 4], P('prompt', 'resp'), may hold values from 0 to 1
Outputs:
- attn_out: bfloat16 [8, 4, 256, 2048], P('prompt', 'resp')
- query_grad: bfloat16 [8, 4, 256, 2048], P('prompt', 'resp')
- key_grad: bfloat16 [8, 4, 256, 512], P('prompt', 'resp')
- value_grad: bfloat16 [8, 4, 256, 512], P('prompt', 'resp')
- prompt_key_gradient: bfloat16 [8, 256, 512], P('prompt', 'resp')
- prompt_value_gradient: bfloat16 [8, 256, 512], P('prompt', 'resp')
The draws below stay inside these ranges and needn't reach their ends.
Inputs may be any that keep to these rules, and one draw needn't show every extreme that they name: `kept_rollout_number`: at least one prompt keeps all 4 responses. `spaces_kept_leading`: each row is an ordering of the 4 slots; the first survivors entries name the surviving slots.
All inputs are finite; a program needn't handle non-finite values.
Results may differ from the reference program's by a relative error of at most 0.012.
The reference program's roundings to bfloat16 on the way count: a program that leaves them out, or rounds other values in their place, can miss the bound.
Values may be sent and summed in bfloat16 or wider, within the bound.
No kernel may reach another device: no remote copies, remote signals or barrier semaphores. Data moves between devices by JAX's collectives and lax.ppermute only.
A program may use at most 64 MiB of HBM per device.

```python
import jax
import jax.numpy as jnp
from jax import lax

QUERY_HEADS = 16
KEY_VALUE_HEADS = 4
HEAD_SIZE = 128
BLOCK = 128
RESP_BLK = 2
RESPONSE_TOKENS = 256
PROMPT_TOKENS = 256
ROLLOUT_SPACES = 4
QUESTION_NUMBER = 8


def draw_answer_asking_tensor(key, part):
    key = jax.random.fold_in(key, 1)
    valid_extent = (QUESTION_NUMBER, ROLLOUT_SPACES, RESPONSE_TOKENS, QUERY_HEADS * HEAD_SIZE)
    sampled_values = jnp.clip(jax.random.normal(key, valid_extent, jnp.float32), -4.0, 4.0)
    return sampled_values.astype(jnp.bfloat16)


def draw_question_lookup_tensor(key, part):
    key = jax.random.fold_in(key, 2)
    valid_extent = (QUESTION_NUMBER, PROMPT_TOKENS, KEY_VALUE_HEADS * HEAD_SIZE)
    sampled_values = jnp.clip(jax.random.normal(key, valid_extent, jnp.float32), -4.0, 4.0)
    return sampled_values.astype(jnp.bfloat16)


def draw_kept_rollout_number(key, part):
    key = jax.random.fold_in(key, 3)
    counts = jax.random.randint(key, (QUESTION_NUMBER,), 2, ROLLOUT_SPACES + 1)
    chosen = jax.random.randint(jax.random.fold_in(key, 1), (), 0, QUESTION_NUMBER)
    counts = jnp.where(jnp.arange(QUESTION_NUMBER) == chosen, ROLLOUT_SPACES, counts)
    return counts.astype(jnp.int32)


def plant(result, stream_key, low, largest):
    shape = result.shape
    place = [jax.random.randint(jax.random.fold_in(stream_key, axis), (), 0, shape[axis]) for axis in range(len(shape))]
    result = result.at[tuple(place)].set(low)
    longest = shape.index(max(shape))
    place[longest] = (place[longest] + 1) % shape[longest]
    return result.at[tuple(place)].set(largest)


def shard_levels(stream_key, shape, split, smallest, high):
    def one(axis_at, parts):
        heights = jax.random.uniform(jax.random.fold_in(jax.random.fold_in(stream_key, 6), axis_at), (parts,), jnp.float32, smallest / len(split), high / len(split))
        return jnp.repeat(jnp.exp(heights), shape[axis_at] // parts).reshape((-1,) + (1,) * (len(shape) - axis_at - 1))

    factor_of = one(*split[0])
    for cut in split[1:]:
        factor_of = factor_of * one(*cut)
    return factor_of


def scatter_about(stream_key, shape, deviation, limit, pieces=(), kind=jnp.bfloat16):
    values = jax.random.normal(stream_key, shape, jnp.float32) * deviation
    if len(pieces) > 0:
        values = shard_levels(stream_key, shape, pieces, -0.22, 0.18) * values
    return jnp.clip(values, min=-limit, max=limit).astype(kind)


def setup_inputs(seed: int = 0) -> dict:
    streams_of = jax.random.split(jax.random.key(seed), 11)
    answer_asking_tensor = draw_answer_asking_tensor(jax.random.fold_in(streams_of[10], 71), 0)
    answer_lookup_tensor = scatter_about(streams_of[1], (QUESTION_NUMBER, ROLLOUT_SPACES, RESPONSE_TOKENS, KEY_VALUE_HEADS * HEAD_SIZE), 1.0, 6.0, ((0, 8), (1, 4)))
    answer_content_tensor = scatter_about(streams_of[2], (QUESTION_NUMBER, ROLLOUT_SPACES, RESPONSE_TOKENS, KEY_VALUE_HEADS * HEAD_SIZE), 1.0, 6.0, ((0, 8), (1, 4)))
    unweighted_mixing_backprop = scatter_about(streams_of[3], (QUESTION_NUMBER, ROLLOUT_SPACES, RESPONSE_TOKENS, QUERY_HEADS * HEAD_SIZE), 1.0, 6.0, ((0, 8), (1, 4)))
    question_lookup_tensor = draw_question_lookup_tensor(jax.random.fold_in(streams_of[10], 71), 0)
    question_content_tensor = scatter_about(streams_of[5], (QUESTION_NUMBER, PROMPT_TOKENS, KEY_VALUE_HEADS * HEAD_SIZE), 1.0, 6.0, ((0, 8), (1, 4)))
    kept_rollout_number = draw_kept_rollout_number(jax.random.fold_in(streams_of[10], 71), 0)
    spaces_kept_leading = jax.vmap(lambda own: jax.random.permutation(own, ROLLOUT_SPACES))(jax.random.split(streams_of[7], QUESTION_NUMBER)).reshape((QUESTION_NUMBER, ROLLOUT_SPACES)).astype(jnp.int32)
    answer_span_tilecounts = plant(jax.random.randint(streams_of[8], (QUESTION_NUMBER, ROLLOUT_SPACES), 1, RESP_BLK + 1), jax.random.fold_in(streams_of[8], 1), 1, RESP_BLK).astype(jnp.int32)
    rollout_payoffs = jnp.clip(1.0 * jax.random.uniform(streams_of[9], (QUESTION_NUMBER, ROLLOUT_SPACES), jnp.float32) ** shard_levels(streams_of[9], (QUESTION_NUMBER, ROLLOUT_SPACES), ((0, 8), (1, 4)), -0.2, 0.2), 0.0, 1.0)
    return {"answer_asking_tensor": answer_asking_tensor, "answer_lookup_tensor": answer_lookup_tensor, "answer_content_tensor": answer_content_tensor, "unweighted_mixing_backprop": unweighted_mixing_backprop, "question_lookup_tensor": question_lookup_tensor, "question_content_tensor": question_content_tensor, "kept_rollout_number": kept_rollout_number, "spaces_kept_leading": spaces_kept_leading, "answer_span_tilecounts": answer_span_tilecounts, "rollout_payoffs": rollout_payoffs}


def respond(query_lines, key_lines, value_lines, gradient_rows, prompt_key_block, prompt_value_block, live_length, slot_weight):
    group_queries = QUERY_HEADS // KEY_VALUE_HEADS
    key_total = PROMPT_TOKENS + RESPONSE_TOKENS
    scaling = HEAD_SIZE ** -0.5
    query_joined = query_lines.astype(jnp.float32).reshape(RESPONSE_TOKENS, KEY_VALUE_HEADS, group_queries, HEAD_SIZE)
    joined_keys = jnp.concatenate([prompt_key_block, key_lines], 0).astype(jnp.float32).reshape(key_total, KEY_VALUE_HEADS, HEAD_SIZE)
    joined_values = jnp.concatenate([prompt_value_block, value_lines], 0).astype(jnp.float32).reshape(key_total, KEY_VALUE_HEADS, HEAD_SIZE)
    scores = jnp.einsum('rkgd,tkd->kgrt', query_joined, joined_keys) * scaling
    row_index = jnp.arange(RESPONSE_TOKENS)[:, None]
    col_index = jnp.arange(key_total)[None, :]
    allowed = (col_index < PROMPT_TOKENS) | (col_index - PROMPT_TOKENS <= row_index)
    scores = jnp.where(allowed, scores, -1e30)
    highest = jnp.max(scores, axis=-1, keepdims=True)
    expo = jnp.exp(scores - highest)
    probs = expo / jnp.sum(expo, axis=-1, keepdims=True)
    probability_lower = probs.astype(jnp.bfloat16).astype(jnp.float32)
    attended = jnp.einsum('kgrt,tkd->rkgd', probability_lower, joined_values)
    is_valid = (jnp.arange(RESPONSE_TOKENS) < live_length)[:, None, None, None]
    attn_out = jnp.where(is_valid, attended, 0.0).astype(jnp.bfloat16).reshape(RESPONSE_TOKENS, QUERY_HEADS * HEAD_SIZE)
    gradient_list = gradient_rows.astype(jnp.float32).reshape(RESPONSE_TOKENS, KEY_VALUE_HEADS, group_queries, HEAD_SIZE) * slot_weight
    output_cotangent = jnp.where(is_valid, gradient_list, 0.0).astype(jnp.bfloat16).astype(jnp.float32)
    probability_grad = jnp.einsum('rkgd,tkd->kgrt', output_cotangent, joined_values)
    delta = jnp.transpose(jnp.sum(output_cotangent * attended, axis=-1), (1, 2, 0))
    score_gradient = (probs * (probability_grad - delta[..., None]) * scaling).astype(jnp.bfloat16).astype(jnp.float32)
    query_grad = jnp.einsum('kgrt,tkd->rkgd', score_gradient, joined_keys).astype(jnp.bfloat16).reshape(RESPONSE_TOKENS, QUERY_HEADS * HEAD_SIZE)
    key_contribution = jnp.einsum('jnlp,ljnu->pju', score_gradient, query_joined).reshape(key_total, KEY_VALUE_HEADS * HEAD_SIZE)
    value_contribution = jnp.einsum('jnlp,ljnu->pju', probability_lower, output_cotangent).reshape(key_total, KEY_VALUE_HEADS * HEAD_SIZE)
    return (attn_out, query_grad, key_contribution[PROMPT_TOKENS:].astype(jnp.bfloat16), value_contribution[PROMPT_TOKENS:].astype(jnp.bfloat16),
            key_contribution[:PROMPT_TOKENS], value_contribution[:PROMPT_TOKENS])


def reference(answer_asking_tensor, answer_lookup_tensor, answer_content_tensor, unweighted_mixing_backprop, question_lookup_tensor, question_content_tensor, kept_rollout_number, spaces_kept_leading, answer_span_tilecounts, rollout_payoffs):
    member_indexes = jnp.arange(ROLLOUT_SPACES)
    numbered_members = member_indexes[None, :] < kept_rollout_number[:, None]
    hits_found = (spaces_kept_leading[:, :, None] == member_indexes[None, None, :]) & numbered_members[:, :, None]
    living = jnp.sum(jnp.where(hits_found, 1, 0), axis=1).astype(jnp.int32)
    live_length = (living * answer_span_tilecounts * BLOCK).astype(jnp.int32)
    surviving_mask_real = living.astype(jnp.float32)
    batch_live = jnp.sum(surviving_mask_real)
    cohort_mean_reward = jnp.sum(surviving_mask_real * rollout_payoffs, axis=1) / kept_rollout_number.astype(jnp.float32)
    slot_weight = (rollout_payoffs - cohort_mean_reward[:, None]) / batch_live

    def per_prompt(inputs):
        query_p, key_p, value_p, grad_p, prompt_key_block, prompt_value_block, length_p, weight_p = inputs

        def per_slot(carry, slot_in):
            query_s, key_s, value_s, grad_s, length_s, weight_s = slot_in
            results = respond(query_s, key_s, value_s, grad_s, prompt_key_block, prompt_value_block, length_s, weight_s)
            carry = (carry[0] + results[4], carry[1] + results[5])
            return carry, results[:4]

        zero_array = jnp.zeros((PROMPT_TOKENS, KEY_VALUE_HEADS * HEAD_SIZE), jnp.float32)
        sums, stacked_arrays = lax.scan(per_slot, (zero_array, zero_array), (query_p, key_p, value_p, grad_p, length_p, weight_p))
        return stacked_arrays + (sums[0].astype(jnp.bfloat16), sums[1].astype(jnp.bfloat16))

    results = lax.map(per_prompt, (answer_asking_tensor, answer_lookup_tensor, answer_content_tensor, unweighted_mixing_backprop, question_lookup_tensor, question_content_tensor, live_length, slot_weight))
    return (results[0], results[1], results[2], results[3], results[4], results[5])
```

```python
import functools
import jax
import jax.numpy as jnp
from jax import lax
from jax.experimental import pallas as pl
from jax.experimental.pallas import tpu as pltpu
from jax.sharding import PartitionSpec as P

HEAD_SIZE = 128
BLOCK = 128
LOG2E = 1.4426950408889634
f32 = jnp.float32
bf16 = jnp.bfloat16


def dot(a, b, ca, cb):
    return lax.dot_general(a, b, (((ca,), (cb,)), ((), ())), preferred_element_type=f32)


def swap(x, axis, n, k):
    return lax.ppermute(x, axis, [(i, i ^ k) for i in range(n)])


def tree_sum(x, axis, n):
    k = 1
    while k < n:
        x = x + swap(x, axis, n, k)
        k *= 2
    return x


def attend_kernel(n, tokens, group, *refs):
    length_ref, weight_ref, q_ref, u_ref, ko_ref, vo_ref = refs[:6]
    kp_refs, vp_refs = refs[6 : 6 + n], refs[6 + n : 6 + 2 * n]
    out_ref, dq_ref, dko_ref, dvo_ref, term_ref = refs[6 + 2 * n :]
    scaling = HEAD_SIZE**-0.5
    weight = weight_ref[0]
    keys = jnp.concatenate([r[...] for r in kp_refs] + [ko_ref[...]], 0)
    values = jnp.concatenate([r[...] for r in vp_refs] + [vo_ref[...]], 0)
    prefix = keys.shape[0] - tokens

    def stack(ref):
        return jnp.concatenate(
            [ref[:, h * HEAD_SIZE : (h + 1) * HEAD_SIZE] for h in range(group)], 0
        )

    def unstack(ref, x):
        for h in range(group):
            ref[:, h * HEAD_SIZE : (h + 1) * HEAD_SIZE] = x[h * tokens : (h + 1) * tokens]

    row = lax.broadcasted_iota(jnp.int32, (tokens, 1), 0)
    valid = jnp.concatenate([row < length_ref[0]] * group, 0)
    causal = lax.broadcasted_iota(jnp.int32, (tokens, tokens), 1) <= row
    causal = jnp.concatenate([causal] * group, 0)

    q = stack(q_ref)
    u = jnp.where(valid, stack(u_ref).astype(f32) * weight, 0.0).astype(bf16)
    s = dot(q, keys, 1, 1)
    s = jnp.concatenate([s[:, :prefix], jnp.where(causal, s[:, prefix:], -1e30)], 1)
    top = jnp.max(s, -1, keepdims=True)
    e = jnp.exp2((s - top) * (scaling * LOG2E))
    p = e * (1.0 / jnp.sum(e, -1, keepdims=True))
    p_low = p.astype(bf16)
    attended = dot(p_low, values, 1, 0)
    unstack(out_ref, jnp.where(valid, attended, 0.0).astype(bf16))
    dp = dot(u, values, 1, 1)
    delta = jnp.sum(u.astype(f32) * attended, -1, keepdims=True)
    ds = (p * (dp - delta) * scaling).astype(bf16)
    unstack(dq_ref, dot(ds, keys, 1, 0).astype(bf16))
    dk = dot(q, ds, 0, 0).T.astype(bf16)
    dv = dot(u, p_low, 0, 0).T.astype(bf16)
    dko_ref[...] = dk[prefix:]
    dvo_ref[...] = dv[prefix:]
    term_ref[0] = dk[:prefix]
    term_ref[1] = dv[:prefix]


def local(q, ko, vo, u, kp, vp, kept, spaces, spans, payoffs):
    n = lax.axis_size("resp")
    n_prompt = lax.axis_size("prompt")
    tokens = q.shape[2]
    kv_heads = ko.shape[3] // HEAD_SIZE
    group = q.shape[3] // ko.shape[3]
    part = kp.shape[1]
    prefix = n * part
    member = lax.axis_index("resp")

    kps = [kp[0]] + [swap(kp, "resp", n, k)[0] for k in range(1, n)]
    vps = [vp[0]] + [swap(vp, "resp", n, k)[0] for k in range(1, n)]

    living = jnp.sum(
        jnp.where((jnp.arange(n) < kept[0]) & (spaces[0] == member), 1, 0)
    ).astype(jnp.int32)
    length = living * spans[0, 0] * BLOCK
    batch_live = tree_sum(kept.astype(f32), "prompt", n_prompt)
    reward_sum = tree_sum(living.astype(f32) * payoffs[0], "resp", n)
    weight = (payoffs[0] - reward_sum / kept.astype(f32)) / batch_live

    def columns(rows, width):
        return pl.BlockSpec((rows, width), lambda g: (0, g))

    scalar = pl.BlockSpec(memory_space=pltpu.SMEM)
    width = group * HEAD_SIZE
    attn_out, dq, dko, dvo, terms = pl.pallas_call(
        functools.partial(attend_kernel, n, tokens, group),
        grid=(kv_heads,),
        in_specs=[scalar, scalar]
        + [columns(tokens, width)] * 2
        + [columns(tokens, HEAD_SIZE)] * 2
        + [columns(part, HEAD_SIZE)] * (2 * n),
        out_specs=[columns(tokens, width)] * 2
        + [columns(tokens, HEAD_SIZE)] * 2
        + [pl.BlockSpec((2, prefix, HEAD_SIZE), lambda g: (0, 0, g))],
        out_shape=[jax.ShapeDtypeStruct(q.shape[2:], bf16)] * 2
        + [jax.ShapeDtypeStruct(ko.shape[2:], bf16)] * 2
        + [jax.ShapeDtypeStruct((2, prefix, kp.shape[2]), bf16)],
        compiler_params=pltpu.CompilerParams(vmem_limit_bytes=56 << 20),
    )(length.reshape(1), weight, q[0, 0], u[0, 0], ko[0, 0], vo[0, 0], *kps, *vps)

    total = terms[:, :part].astype(f32)
    for k in range(1, n):
        total += swap(terms[:, k * part : (k + 1) * part], "resp", n, k).astype(f32)
    total = total.astype(bf16)
    return (
        attn_out[None, None],
        dq[None, None],
        dko[None, None],
        dvo[None, None],
        total[:1],
        total[1:],
    )


def solution(mesh):
    wide = P("prompt", "resp", None, None)
    rows = P("prompt", "resp", None)
    pair = P("prompt", "resp")
    return jax.shard_map(
        local,
        mesh=mesh,
        in_specs=(wide, wide, wide, wide, rows, rows, P("prompt"), P("prompt", None), pair, pair),
        out_specs=(wide, wide, wide, wide, rows, rows),
        check_vma=False,
    )
```

```python
import functools
import jax
import jax.numpy as jnp
from jax import lax
from jax.experimental import pallas as pl
from jax.experimental.pallas import tpu as pltpu
from jax.sharding import PartitionSpec as P

HEAD_SIZE = 128
BLOCK = 128
EXTRA = 16
SCALING = HEAD_SIZE**-0.5
POWER = SCALING * 1.4426950408889634
f32 = jnp.float32
bf16 = jnp.bfloat16


def dot(a, b, ca, cb):
    return lax.dot_general(a, b, (((ca,), (cb,)), ((), ())), preferred_element_type=f32)


def swap(x, n, k):
    return lax.ppermute(x, "resp", [(i, i ^ k) for i in range(n)])


def stack(ref, group):
    return jnp.concatenate([ref[:, h * HEAD_SIZE : (h + 1) * HEAD_SIZE] for h in range(group)], 0)


def unstack(ref, x, group):
    tokens = ref.shape[0]
    for h in range(group):
        ref[:, h * HEAD_SIZE : (h + 1) * HEAD_SIZE] = x[h * tokens : (h + 1) * tokens]


def causal_mask(tokens, group):
    row = lax.broadcasted_iota(jnp.int32, (tokens, tokens), 0)
    col = lax.broadcasted_iota(jnp.int32, (tokens, tokens), 1)
    return jnp.concatenate([col <= row] * group, 0)


def survives(spaces_ref, kept_ref, member):
    hits = [
        jnp.where((i < kept_ref[0]) & (spaces_ref[0, i] == member), 1, 0)
        for i in range(spaces_ref.shape[1])
    ]
    return sum(hits)


def valid_rows(spaces_ref, kept_ref, spans_ref, member, tokens, group):
    length = survives(spaces_ref, kept_ref, member) * spans_ref[0, 0] * BLOCK
    row = lax.broadcasted_iota(jnp.int32, (tokens, 1), 0)
    return jnp.concatenate([row < length] * group, 0)


def own_kernel(group, counts, *refs):
    count_refs, (q_ref, ko_ref, vo_ref, att_ref, stat_ref, part_ref) = refs[:counts], refs[counts:]
    part_ref[0] = sum(r[0] for r in count_refs)
    tokens = q_ref.shape[0]
    s = dot(stack(q_ref, group), ko_ref[...], 1, 1)
    s = jnp.where(causal_mask(tokens, group), s, -1e30)
    top = jnp.max(s, -1, keepdims=True)
    e = jnp.exp2((s - top) * POWER)
    stat_ref[0, :, 0:1] = top
    stat_ref[0, :, 1:2] = jnp.sum(e, -1, keepdims=True)
    att_ref[0] = dot(e.astype(bf16), vo_ref[...], 1, 0)


def prefix_kernel(n, group, *refs):
    (place_ref, kept_ref, spaces_ref, spans_ref, payoff_ref, part_ref, recv_ref) = refs[:7]
    q_ref, u_ref, own_ref, stat_ref = refs[7:11]
    kp_refs, vp_refs = refs[11 : 11 + n], refs[11 + n : 11 + 2 * n]
    pay_refs = refs[11 + 2 * n : 10 + 3 * n]
    out_ref, ds_ref, line_ref, weight_ref, sum_ref = refs[10 + 3 * n : 15 + 3 * n]
    term_refs = refs[15 + 3 * n :]
    tokens = q_ref.shape[0]
    part = kp_refs[0].shape[0]
    member = place_ref[0]
    sum_ref[0] = part_ref[0] + recv_ref[0]

    total = jnp.where(survives(spaces_ref, kept_ref, member) > 0, payoff_ref[0, 0], 0.0)
    total = jnp.full((1, 1), total, f32)
    for k in range(1, n):
        pieces = pay_refs[k - 1][...].astype(f32)
        reward = pieces[0:1, 0:1] + pieces[1:2, 0:1] + pieces[2:3, 0:1]
        total += jnp.where(survives(spaces_ref, kept_ref, member ^ k) > 0, reward, 0.0)
    weight = payoff_ref[0, 0] - total / kept_ref[0].astype(f32)
    weight_ref[...] = jnp.broadcast_to(weight, weight_ref.shape)

    keys = jnp.concatenate([r[...] for r in kp_refs], 0)
    values = jnp.concatenate([r[...] for r in vp_refs], 0)
    valid = valid_rows(spaces_ref, kept_ref, spans_ref, member, tokens, group)
    q = stack(q_ref, group)
    u = jnp.where(valid, stack(u_ref, group), 0.0)
    s = dot(q, keys, 1, 1)
    own_top = stat_ref[0, :, 0:1]
    top = jnp.maximum(jnp.max(s, -1, keepdims=True), own_top)
    e = jnp.exp2((s - top) * POWER)
    shrink = jnp.exp2((own_top - top) * POWER)
    mass = jnp.sum(e, -1, keepdims=True) + shrink * stat_ref[0, :, 1:2]
    inverse = 1.0 / mass
    p = e * inverse
    p_low = p.astype(bf16)
    attended = dot(p_low, values, 1, 0) + own_ref[0] * (shrink * inverse)
    unstack(out_ref, jnp.where(valid, attended, 0.0).astype(bf16), group)
    dp = dot(u, values, 1, 1)
    delta = jnp.sum(u.astype(f32) * attended, -1, keepdims=True)
    ds = (p * (dp - delta)).astype(bf16)
    ds_ref[0] = ds
    line_ref[0, :, 0:1] = top * POWER + jnp.log2(mass)
    line_ref[0, :, 1:2] = delta
    dk = dot(q, ds, 0, 0).T * (weight * SCALING)
    dv = dot(u, p_low, 0, 0).T * weight
    for k, ref in enumerate(term_refs):
        ref[0] = dk[k * part : (k + 1) * part].astype(ref.dtype)
        ref[1] = dv[k * part : (k + 1) * part].astype(ref.dtype)


def rest_kernel(n, group, *refs):
    (place_ref, kept_ref, spaces_ref, spans_ref, sum_ref, recv_ref) = refs[:6]
    weight_ref, q_ref, u_ref, ko_ref, vo_ref, ds_ref, line_ref = refs[6:13]
    kp_refs = refs[13 : 13 + n]
    dq_ref, dko_ref, dvo_ref = refs[13 + n :]
    tokens = q_ref.shape[0]
    batch = (sum_ref[0] + recv_ref[0]).astype(f32)
    weight = weight_ref[0:1, 0:1] / batch
    keys = jnp.concatenate([r[...] for r in kp_refs], 0)
    valid = valid_rows(spaces_ref, kept_ref, spans_ref, place_ref[0], tokens, group)
    q = stack(q_ref, group)
    u = jnp.where(valid, stack(u_ref, group), 0.0)
    s = dot(q, ko_ref[...], 1, 1)
    s = jnp.where(causal_mask(tokens, group), s, -1e30)
    p = jnp.exp2(s * POWER - line_ref[0, :, 0:1])
    dp = dot(u, vo_ref[...], 1, 1)
    ds = (p * (dp - line_ref[0, :, 1:2])).astype(bf16)
    dq = dot(ds_ref[0], keys, 1, 0) + dot(ds, ko_ref[...], 1, 0)
    unstack(dq_ref, (dq * (weight * SCALING)).astype(bf16), group)
    dko_ref[...] = (dot(q, ds, 0, 0).T * (weight * SCALING)).astype(bf16)
    dvo_ref[...] = (dot(u, p.astype(bf16), 0, 0).T * weight).astype(bf16)


def local(q, ko, vo, u, kp, vp, kept, spaces, spans, payoffs):
    n = lax.axis_size("resp")
    n_prompt = lax.axis_size("prompt")
    tokens = q.shape[2]
    kv_width = ko.shape[3]
    kv_heads = kv_width // HEAD_SIZE
    group = q.shape[3] // kv_width
    width = group * HEAD_SIZE
    rows = group * tokens
    part = kp.shape[1]
    prefix = n * part
    q, ko, vo, u = q[0, 0], ko[0, 0], vo[0, 0], u[0, 0]
    place = lax.axis_index("resp").astype(jnp.int32).reshape(1)

    high = payoffs.astype(bf16)
    middle = (payoffs - high.astype(f32)).astype(bf16)
    low = (payoffs - high.astype(f32) - middle.astype(f32)).astype(bf16)
    pieces = jnp.concatenate([high, middle, low, jnp.zeros((EXTRA - 3, 1), bf16)], 0)
    payload = jnp.concatenate([kp[0], vp[0], jnp.broadcast_to(pieces, (EXTRA, kv_width))], 0)
    arrived = [swap(payload, n, k) for k in range(1, n)]

    share = -(-n_prompt // n)
    counts = []
    for a in range(share):
        perm = [
            (p * n + m, (p ^ (m * share + a)) * n + m)
            for p in range(n_prompt)
            for m in range(n)
            if m * share + a < n_prompt
        ]
        counts.append(lax.ppermute(kept, ("prompt", "resp"), perm))

    scalar = pl.BlockSpec(memory_space=pltpu.SMEM)
    one = jax.ShapeDtypeStruct((1,), jnp.int32)

    def columns(height, width, at=0):
        return pl.BlockSpec((height, width), lambda g: (at, g))

    def head(height, width):
        return pl.BlockSpec((1, height, width), lambda g: (g, 0, 0))

    def call(kernel, units, in_specs, out, args):
        return pl.pallas_call(
            kernel,
            grid=(kv_heads,),
            in_specs=in_specs,
            out_specs=[spec for spec, _ in out],
            out_shape=[shape for _, shape in out],
            compiler_params=pltpu.CompilerParams(vmem_limit_bytes=48 << 20),
            cost_estimate=pl.CostEstimate(
                flops=units * 2 * kv_heads * rows * tokens * HEAD_SIZE,
                bytes_accessed=4 << 20,
                transcendentals=kv_heads * rows * tokens,
            ),
        )(*args)

    def shaped(shape, kind):
        return jax.ShapeDtypeStruct(shape, kind)

    stat = (head(rows, 2), shaped((kv_heads, rows, 2), f32))
    wide, slim = columns(tokens, width), columns(tokens, HEAD_SIZE)

    own, own_stat, part_sum = call(
        functools.partial(own_kernel, group, share),
        2,
        [scalar] * share + [wide, slim, slim],
        [(head(rows, HEAD_SIZE), shaped((kv_heads, rows, HEAD_SIZE), f32)), stat, (scalar, one)],
        (*counts, q, ko, vo),
    )
    k = 1
    while 4 * k < n:
        part_sum = part_sum + swap(part_sum, n, k)
        k *= 2
    key_specs = [columns(part, HEAD_SIZE)] * n
    keys = [kp[0]] + arrived
    attn_out, ds, line, weight, batch, *terms = call(
        functools.partial(prefix_kernel, n, group),
        5,
        [scalar] * 7
        + [wide, wide, head(rows, HEAD_SIZE), head(rows, 2)]
        + key_specs
        + [columns(part, HEAD_SIZE)]
        + [columns(part, HEAD_SIZE, 1)] * (n - 1)
        + [pl.BlockSpec((EXTRA, HEAD_SIZE), lambda g: (2 * part // EXTRA, 0))] * (n - 1),
        [
            (wide, shaped(q.shape, bf16)),
            (head(rows, prefix), shaped((kv_heads, rows, prefix), bf16)),
            stat,
            (pl.BlockSpec((8, HEAD_SIZE), lambda g: (0, 0)), shaped((8, HEAD_SIZE), f32)),
            (scalar, one),
        ]
        + [
            (
                pl.BlockSpec((2, part, HEAD_SIZE), lambda g: (0, 0, g)),
                shaped((2, part, kv_width), f32 if i == 0 else bf16),
            )
            for i in range(n)
        ],
        (place, kept, spaces, spans, payoffs, part_sum, swap(part_sum, n, k))
        + (q, u, own, own_stat, *keys, vp[0], *arrived, *arrived),
    )
    other = swap(batch, n, 2 * k)
    received = [swap(t, n, i) for i, t in enumerate(terms) if i > 0]
    dq, dko, dvo = call(
        functools.partial(rest_kernel, n, group),
        6,
        [scalar] * 6
        + [pl.BlockSpec((8, HEAD_SIZE), lambda g: (0, 0))]
        + [wide, wide, slim, slim, head(rows, prefix), head(rows, 2)]
        + key_specs,
        [(wide, shaped(q.shape, bf16))] + [(slim, shaped(ko.shape, bf16))] * 2,
        (place, kept, spaces, spans, batch, other, weight, q, u, ko, vo, ds, line, *keys),
    )
    total = terms[0]
    for t in received:
        total += t.astype(f32)
    total = (total / (batch + other).astype(f32)).astype(bf16)
    return (
        attn_out[None, None],
        dq[None, None],
        dko[None, None],
        dvo[None, None],
        total[:1],
        total[1:],
    )


def solution(mesh):
    wide = P("prompt", "resp", None, None)
    rows = P("prompt", "resp", None)
    pair = P("prompt", "resp")
    return jax.shard_map(
        local,
        mesh=mesh,
        in_specs=(wide, wide, wide, wide, rows, rows, P("prompt"), P("prompt", None), pair, pair),
        out_specs=(wide, wide, wide, wide, rows, rows),
        check_vma=False,
    )
```

```python
import functools
import jax
import jax.numpy as jnp
from jax import lax
from jax.experimental import pallas as pl
from jax.experimental.pallas import tpu as pltpu
from jax.sharding import PartitionSpec as P

HEAD_SIZE = 128
BLOCK = 128
SCALING = HEAD_SIZE**-0.5
POWER = SCALING * 1.4426950408889634
VMEM_LIMIT = 32 << 20
f32 = jnp.float32
bf16 = jnp.bfloat16
i32 = jnp.int32


def dot(a, b, ca, cb):
    return lax.dot_general(a, b, (((ca,), (cb,)), ((), ())), preferred_element_type=f32)


def swap(x, n, k):
    return lax.ppermute(x, "resp", [(i, i ^ k) for i in range(n)])


def columns_of(g, width):
    return pl.ds(pl.multiple_of(g * width, width), width)


def stacked(block):
    width = block.shape[1]
    return jnp.concatenate([block[:, i : i + HEAD_SIZE] for i in range(0, width, HEAD_SIZE)], 0)


def unstacked(x, tokens):
    x = x.astype(bf16)
    return jnp.concatenate([x[:, i : i + tokens].T for i in range(0, x.shape[1], tokens)], 1)


def causal_mask(tokens, group):
    key = lax.broadcasted_iota(i32, (tokens, tokens), 0)
    row = lax.broadcasted_iota(i32, (tokens, tokens), 1)
    return jnp.concatenate([key <= row] * group, 1)


def row_of(tile, index):
    row = lax.broadcasted_iota(i32, tile.shape, 0)
    return jnp.sum(jnp.where(row == index, tile, 0.0), 0, keepdims=True)


def pack_kernel(kp_hbm, vp_hbm, payload_ref, sems):
    part = kp_hbm.shape[0]
    copies = [
        pltpu.make_async_copy(kp_hbm, payload_ref.at[:part], sems.at[0, 0]),
        pltpu.make_async_copy(vp_hbm, payload_ref.at[part:], sems.at[1, 0]),
    ]
    for copy in copies:
        copy.start()
    for copy in copies:
        copy.wait()


def own_kernel(n, group, counts, *refs):
    small_hbm, refs = refs[: 4 + counts], refs[4 + counts :]
    q_hbm, u_hbm, ko_hbm, vo_hbm = refs[:4]
    q_ref, u_ref, ko_ref, vo_ref, att_ref, stat_ref, tile_ref, alive_ref = refs[4:12]
    small_refs, sems, small_sems = refs[12:-2], refs[-2], refs[-1]
    heads, tokens, width = q_ref.shape

    def loads(g):
        return [
            pltpu.make_async_copy(ko_hbm.at[:, columns_of(g, HEAD_SIZE)], ko_ref.at[g], sems.at[0, g]),
            pltpu.make_async_copy(q_hbm.at[:, columns_of(g, width)], q_ref.at[g], sems.at[1, g]),
            pltpu.make_async_copy(vo_hbm.at[:, columns_of(g, HEAD_SIZE)], vo_ref.at[g], sems.at[2, g]),
        ]

    def late_load(g):
        return pltpu.make_async_copy(u_hbm.at[:, columns_of(g, width)], u_ref.at[g], sems.at[3, g])

    small = [
        pltpu.make_async_copy(a, b, small_sems.at[i])
        for i, (a, b) in enumerate(zip(small_hbm, small_refs))
    ]
    for copy in small:
        copy.start()
    for g in range(heads):
        for copy in loads(g):
            copy.start()
    for g in range(heads):
        late_load(g).start()

    for copy in small:
        copy.wait()
    kept_ref, spaces_ref, spans_ref, payoff_ref = small_refs[:4]
    member = lax.axis_index("resp")
    kept = kept_ref[0]
    row = lax.broadcasted_iota(i32, tile_ref.shape, 0)
    alive = jnp.zeros(tile_ref.shape, f32)
    own_alive = 0
    for i in range(spaces_ref.shape[1]):
        alive += jnp.where((row == spaces_ref[0, i]) & (i < kept), 1.0, 0.0)
        own_alive += jnp.where((spaces_ref[0, i] == member) & (i < kept), 1, 0)
    alive_ref[...] = alive
    count = sum(r[0] for r in small_refs[4:]).astype(f32)
    tile_ref[...] = jnp.where(row == member, payoff_ref[0, 0], 0.0) + jnp.where(row == n, count, 0.0)
    token = lax.broadcasted_iota(i32, (1, tokens), 1)
    valid = jnp.where(token < own_alive * spans_ref[0, 0] * BLOCK, 1.0, 0.0)
    valid = jnp.concatenate([valid] * group, 1)

    def step(g, carry):
        for copy in loads(g):
            copy.wait()
        s = dot(ko_ref[g], stacked(q_ref[g]), 1, 1)
        s = jnp.where(causal_mask(tokens, group), s, -1e30)
        top = jnp.max(s, 0, keepdims=True)
        e = jnp.exp2((s - top) * POWER)
        stat_ref[g, 0:1] = top
        stat_ref[g, 1:2] = jnp.sum(e, 0, keepdims=True)
        stat_ref[g, 2:3] = valid
        att_ref[g] = dot(vo_ref[g], e.astype(bf16), 0, 0)
        return carry

    lax.fori_loop(0, heads, step, 0)
    for g in range(heads):
        late_load(g).wait()


def prefix_kernel(n, *refs):
    q_ref, u_ref, own_ref, stat_ref, tile_ref, recv_ref = refs[:6]
    pay_refs = refs[6 : 6 + n]
    out_ref, ds_ref, line_ref, sum_ref = refs[6 + n : 10 + n]
    term_refs = refs[10 + n :]
    heads, tokens, width = q_ref.shape
    part = pay_refs[0].shape[0] // 2
    sum_ref[...] = tile_ref[...] + recv_ref[...]

    def step(g, carry):
        cols = columns_of(g, HEAD_SIZE)
        keys = jnp.concatenate([r[:part, cols] for r in pay_refs], 0)
        values = jnp.concatenate([r[part:, cols] for r in pay_refs], 0)
        q = stacked(q_ref[g])
        u = stacked(u_ref[g])
        s = dot(keys, q, 1, 1)
        own_top = stat_ref[g, 0:1]
        valid = stat_ref[g, 2:3] > 0.0
        top = jnp.maximum(jnp.max(s, 0, keepdims=True), own_top)
        e = jnp.exp2((s - top) * POWER)
        shrink = jnp.exp2((own_top - top) * POWER)
        mass = jnp.sum(e, 0, keepdims=True) + shrink * stat_ref[g, 1:2]
        inverse = jnp.where(valid, 1.0 / mass, 0.0)
        p = e * inverse
        p_low = p.astype(bf16)
        attended = dot(values, p_low, 0, 0) + own_ref[g] * (shrink * inverse)
        out_ref[g] = unstacked(attended, tokens)
        dp = dot(values, u, 1, 1)
        delta = jnp.sum(u.T.astype(f32) * attended, 0, keepdims=True)
        ds = (p * (dp - delta)).astype(bf16)
        ds_ref[g] = ds
        line_ref[g, 0:1] = jnp.where(valid, top * POWER + jnp.log2(mass), 1e30)
        line_ref[g, 1:2] = delta
        dk = dot(ds, q, 1, 0) * SCALING
        dv = dot(p_low, u, 1, 0)
        for k, ref in enumerate(term_refs):
            ref[:part, cols] = dk[k * part : (k + 1) * part].astype(ref.dtype)
            ref[part:, cols] = dv[k * part : (k + 1) * part].astype(ref.dtype)
        return carry

    lax.fori_loop(0, heads, step, 0)


def rest_kernel(n, group, *refs):
    q_ref, u_ref, ko_ref, vo_ref, att_ref, ds_ref, line_ref, sum_ref, recv_ref, alive_ref = refs[:10]
    pay_refs = refs[10 : 10 + n]
    out_hbm, dq_hbm, dko_hbm, dvo_hbm, weights_ref = refs[10 + n : 15 + n]
    dq_ref, dko_ref, dvo_ref, sems = refs[15 + n :]
    heads, tokens, width = q_ref.shape
    part = pay_refs[0].shape[0] // 2

    def early_store(g):
        return pltpu.make_async_copy(att_ref.at[g], out_hbm.at[:, columns_of(g, width)], sems.at[0, g])

    def stores(g):
        slim = columns_of(g, HEAD_SIZE)
        return [
            pltpu.make_async_copy(dq_ref.at[g], dq_hbm.at[:, columns_of(g, width)], sems.at[1, g]),
            pltpu.make_async_copy(dko_ref.at[g], dko_hbm.at[:, slim], sems.at[2, g]),
            pltpu.make_async_copy(dvo_ref.at[g], dvo_hbm.at[:, slim], sems.at[3, g]),
        ]

    for g in range(heads):
        early_store(g).start()
    tile = sum_ref[...] + recv_ref[...]
    alive = alive_ref[...]
    mean = jnp.sum(tile * alive, 0, keepdims=True) / jnp.sum(alive, 0, keepdims=True)
    weights = (tile - mean) / row_of(tile, n)
    weights_ref[...] = weights
    weight = row_of(weights, lax.axis_index("resp"))
    weight_rows = jnp.concatenate([weight] * (group * tokens // HEAD_SIZE), 1)

    def step(g, carry):
        cols = columns_of(g, HEAD_SIZE)
        keys = jnp.concatenate([r[:part, cols] for r in pay_refs], 0)
        q = stacked(q_ref[g])
        u = stacked(u_ref[g])
        ko, vo = ko_ref[g], vo_ref[g]
        s = dot(ko, q, 1, 1)
        s = jnp.where(causal_mask(tokens, group), s, -1e30)
        p = jnp.exp2(s * POWER - line_ref[g, 0:1])
        dp = dot(vo, u, 1, 1)
        ds = (p * (dp - line_ref[g, 1:2])).astype(bf16)
        dq = dot(keys, ds_ref[g], 0, 0) + dot(ko, ds, 0, 0)
        dq_ref[g] = unstacked(dq * (weight_rows * SCALING), tokens)
        dko_ref[g] = (dot(ds, q, 1, 0) * (weight * SCALING)).astype(bf16)
        dvo_ref[g] = (dot(p.astype(bf16), u, 1, 0) * weight).astype(bf16)
        for copy in stores(g):
            copy.start()
        return carry

    lax.fori_loop(0, heads, step, 0)
    for g in range(heads):
        early_store(g).wait()
        for copy in stores(g):
            copy.wait()


def total_kernel(n, weights_ref, *refs):
    term_refs, (key_ref, value_ref) = refs[:n], refs[n:]
    part, width = key_ref.shape
    weights = weights_ref[...]
    member = lax.axis_index("resp")
    total = jnp.zeros((2 * part, width), f32)
    for k, ref in enumerate(term_refs):
        weight = row_of(weights, member ^ k)
        total += ref[...].astype(f32) * jnp.concatenate([weight] * (width // HEAD_SIZE), 1)
    key_ref[...] = total[:part].astype(bf16)
    value_ref[...] = total[part:].astype(bf16)


def local(q, ko, vo, u, kp, vp, kept, spaces, spans, payoffs):
    n = lax.axis_size("resp")
    n_prompt = lax.axis_size("prompt")
    tokens = q.shape[2]
    kv_width = ko.shape[3]
    heads = kv_width // HEAD_SIZE
    group = q.shape[3] // kv_width
    width = group * HEAD_SIZE
    rows = group * tokens
    part = kp.shape[1]
    prefix = n * part
    tile_shape = (-(-(n + 1) // 8) * 8, HEAD_SIZE)

    vmem = pl.BlockSpec(memory_space=pltpu.VMEM)
    hbm = pl.BlockSpec(memory_space=pl.ANY)

    def pinned(x):
        return pltpu.with_memory_space_constraint(x, pltpu.HBM)

    def call(kernel, units, ins, out, scratch):
        return pl.pallas_call(
            kernel,
            in_specs=[spec for spec, _ in ins],
            out_specs=[spec for spec, _ in out],
            out_shape=[shape for _, shape in out],
            scratch_shapes=scratch,
            compiler_params=pltpu.CompilerParams(vmem_limit_bytes=VMEM_LIMIT),
            cost_estimate=pl.CostEstimate(
                flops=units * 2 * heads * rows * tokens * HEAD_SIZE,
                bytes_accessed=1 << 20,
                transcendentals=0,
            ),
        )(*[x for _, x in ins])

    def kept_in(shape, kind):
        return (vmem, pltpu.VMEM(shape, kind))

    def given(shape, kind=bf16, spec=hbm):
        return (spec, jax.ShapeDtypeStruct(shape, kind))

    sems = pltpu.SemaphoreType.DMA((4, heads))
    stat = kept_in((heads, 8, rows), f32)
    tile_kind = kept_in(tile_shape, f32)
    wide, slim = (heads, tokens, width), (heads, tokens, HEAD_SIZE)
    q, ko, vo, u = q[0, 0], ko[0, 0], vo[0, 0], u[0, 0]

    (payload,) = call(
        pack_kernel,
        0,
        [(hbm, pinned(kp[0])), (hbm, pinned(vp[0]))],
        [kept_in((2 * part, kv_width), bf16)],
        [sems],
    )
    pays = [payload] + [swap(payload, n, k) for k in range(1, n)]

    share = -(-n_prompt // n)
    counts = []
    for a in range(share):
        perm = [
            (p * n + m, (p ^ (m * share + a)) * n + m)
            for p in range(n_prompt)
            for m in range(n)
            if m * share + a < n_prompt
        ]
        counts.append(lax.ppermute(kept, ("prompt", "resp"), perm))

    small = [kept, spaces, spans, payoffs] + counts
    q_in, u_in, ko_in, vo_in, own, own_stat, tile, alive = call(
        functools.partial(own_kernel, n, group, share),
        2,
        [(hbm, x) for x in small] + [(hbm, pinned(x)) for x in (q, u, ko, vo)],
        [kept_in(wide, bf16)] * 2
        + [kept_in(slim, bf16)] * 2
        + [kept_in((heads, HEAD_SIZE, rows), f32), stat, tile_kind, tile_kind],
        [pltpu.SMEM(x.shape, x.dtype) for x in small]
        + [sems, pltpu.SemaphoreType.DMA((len(small),))],
    )
    k = 1
    while 4 * k < n:
        tile = tile + swap(tile, n, k)
        k *= 2
    att, ds, line, tile_sum, *terms = call(
        functools.partial(prefix_kernel, n),
        5,
        [(vmem, x) for x in [q_in, u_in, own, own_stat, tile, swap(tile, n, k)] + pays],
        [kept_in(wide, bf16), kept_in((heads, prefix, rows), bf16), stat, tile_kind]
        + [kept_in((2 * part, kv_width), f32 if i == 0 else bf16) for i in range(n)],
        [],
    )
    other = swap(tile_sum, n, 2 * k)
    received = [swap(t, n, i) for i, t in enumerate(terms) if i > 0]
    attn_out, dq, dko, dvo, weights = call(
        functools.partial(rest_kernel, n, group),
        6,
        [(vmem, x) for x in [q_in, u_in, ko_in, vo_in, att, ds, line, tile_sum, other, alive] + pays],
        [given(q.shape), given(q.shape), given(ko.shape), given(ko.shape), tile_kind],
        [pltpu.VMEM(wide, bf16), pltpu.VMEM(slim, bf16), pltpu.VMEM(slim, bf16), sems],
    )
    key_total, value_total = call(
        functools.partial(total_kernel, n),
        0,
        [(vmem, x) for x in [weights, terms[0]] + received],
        [given((part, kv_width), spec=vmem)] * 2,
        [],
    )
    return (
        attn_out[None, None],
        dq[None, None],
        dko[None, None],
        dvo[None, None],
        key_total[None],
        value_total[None],
    )


def solution(mesh):
    wide = P("prompt", "resp", None, None)
    rows = P("prompt", "resp", None)
    pair = P("prompt", "resp")
    return jax.shard_map(
        local,
        mesh=mesh,
        in_specs=(wide, wide, wide, wide, rows, rows, P("prompt"), P("prompt", None), pair, pair),
        out_specs=(wide, wide, wide, wide, rows, rows),
        check_vma=False,
    )
```

```python
import functools
import jax
import jax.numpy as jnp
from jax import lax
from jax.experimental import pallas as pl
from jax.experimental.pallas import tpu as pltpu
from jax.sharding import PartitionSpec as P

HEAD_SIZE = 128
BLOCK = 128
EXTRA = 16
SCALING = HEAD_SIZE**-0.5
POWER = SCALING * 1.4426950408889634
VMEM_LIMIT = 32 << 20
f32 = jnp.float32
bf16 = jnp.bfloat16
i32 = jnp.int32


def dot(a, b, ca, cb):
    return lax.dot_general(a, b, (((ca,), (cb,)), ((), ())), preferred_element_type=f32)


def swap(x, n, k):
    return lax.ppermute(x, "resp", [(i, i ^ k) for i in range(n)])


def columns_of(g, width):
    return pl.ds(pl.multiple_of(g * width, width), width)


def stacked(block):
    width = block.shape[1]
    return jnp.concatenate([block[:, i : i + HEAD_SIZE] for i in range(0, width, HEAD_SIZE)], 0)


def unstacked(x, tokens):
    x = x.astype(bf16)
    return jnp.concatenate([x[:, i : i + tokens].T for i in range(0, x.shape[1], tokens)], 1)


def causal_mask(tokens, group):
    key = lax.broadcasted_iota(i32, (tokens, tokens), 0)
    row = lax.broadcasted_iota(i32, (tokens, tokens), 1)
    return jnp.concatenate([key <= row] * group, 1)


def row_of(tile, index):
    row = lax.broadcasted_iota(i32, tile.shape, 0)
    return jnp.sum(jnp.where(row == index, tile, 0.0), 0, keepdims=True)


def pack_kernel(payoff_ref, kp_hbm, vp_hbm, payload_ref, sems):
    part, width = kp_hbm.shape
    copies = [
        pltpu.make_async_copy(kp_hbm, payload_ref.at[:part], sems.at[0, 0]),
        pltpu.make_async_copy(vp_hbm, payload_ref.at[part : 2 * part], sems.at[1, 0]),
    ]
    for copy in copies:
        copy.start()
    payoff = jnp.full((EXTRA, width), payoff_ref[0, 0], f32)
    high = payoff.astype(bf16).astype(f32)
    middle = (payoff - high).astype(bf16).astype(f32)
    low = payoff - high - middle
    row = lax.broadcasted_iota(i32, payoff.shape, 0)
    pieces = jnp.where(row == 0, high, jnp.where(row == 1, middle, jnp.where(row == 2, low, 0.0)))
    payload_ref[2 * part :] = pieces.astype(bf16)
    for copy in copies:
        copy.wait()


def own_kernel(group, counts, *refs):
    small_hbm, refs = refs[: 3 + counts], refs[3 + counts :]
    q_hbm, u_hbm, ko_hbm, vo_hbm = refs[:4]
    q_ref, u_ref, ko_ref, vo_ref, att_ref, stat_ref, tile_ref, alive_ref = refs[4:12]
    small_refs, sems, small_sems = refs[12:-2], refs[-2], refs[-1]
    heads, tokens, width = q_ref.shape

    def loads(g):
        return [
            pltpu.make_async_copy(ko_hbm.at[:, columns_of(g, HEAD_SIZE)], ko_ref.at[g], sems.at[0, g]),
            pltpu.make_async_copy(q_hbm.at[:, columns_of(g, width)], q_ref.at[g], sems.at[1, g]),
            pltpu.make_async_copy(vo_hbm.at[:, columns_of(g, HEAD_SIZE)], vo_ref.at[g], sems.at[2, g]),
        ]

    def late_load(g):
        return pltpu.make_async_copy(u_hbm.at[:, columns_of(g, width)], u_ref.at[g], sems.at[3, g])

    small = [
        pltpu.make_async_copy(a, b, small_sems.at[i])
        for i, (a, b) in enumerate(zip(small_hbm, small_refs))
    ]
    for copy in small:
        copy.start()
    for g in range(heads):
        for copy in loads(g):
            copy.start()
    for g in range(heads):
        late_load(g).start()

    for copy in small:
        copy.wait()
    kept_ref, spaces_ref, spans_ref = small_refs[:3]
    member = lax.axis_index("resp")
    kept = kept_ref[0]
    row = lax.broadcasted_iota(i32, alive_ref.shape, 0)
    alive = jnp.zeros(alive_ref.shape, f32)
    own_alive = 0
    for i in range(spaces_ref.shape[1]):
        alive += jnp.where((row == spaces_ref[0, i]) & (i < kept), 1.0, 0.0)
        own_alive += jnp.where((spaces_ref[0, i] == member) & (i < kept), 1, 0)
    alive_ref[...] = alive
    count = kept + sum(r[0] for r in small_refs[3:])
    tile_ref[...] = jnp.full(tile_ref.shape, count.astype(f32))
    token = lax.broadcasted_iota(i32, (1, tokens), 1)
    valid = jnp.where(token < own_alive * spans_ref[0, 0] * BLOCK, 1.0, 0.0)
    valid = jnp.concatenate([valid] * group, 1)

    def step(g, carry):
        for copy in loads(g):
            copy.wait()
        s = dot(ko_ref[g], stacked(q_ref[g]), 1, 1)
        s = jnp.where(causal_mask(tokens, group), s, -1e30)
        top = jnp.max(s, 0, keepdims=True)
        e = jnp.exp2((s - top) * POWER)
        stat_ref[g, 0:1] = top
        stat_ref[g, 1:2] = jnp.sum(e, 0, keepdims=True)
        stat_ref[g, 2:3] = valid
        att_ref[g] = dot(vo_ref[g], e.astype(bf16), 0, 0)
        return carry

    lax.fori_loop(0, heads, step, 0)
    for g in range(heads):
        late_load(g).wait()


def prefix_kernel(n, *refs):
    q_ref, u_ref, own_ref, stat_ref, tile_ref, recv_ref = refs[:6]
    pay_refs = refs[6 : 6 + n]
    out_ref, ds_ref, line_ref, sum_ref = refs[6 + n : 10 + n]
    term_refs = refs[10 + n :]
    heads, tokens, width = q_ref.shape
    part = (pay_refs[0].shape[0] - EXTRA) // 2
    sum_ref[...] = tile_ref[...] + recv_ref[...]

    def step(g, carry):
        cols = columns_of(g, HEAD_SIZE)
        keys = jnp.concatenate([r[:part, cols] for r in pay_refs], 0)
        values = jnp.concatenate([r[part : 2 * part, cols] for r in pay_refs], 0)
        q = stacked(q_ref[g])
        u = stacked(u_ref[g])
        s = dot(keys, q, 1, 1)
        own_top = stat_ref[g, 0:1]
        valid = stat_ref[g, 2:3] > 0.0
        top = jnp.maximum(jnp.max(s, 0, keepdims=True), own_top)
        e = jnp.exp2((s - top) * POWER)
        shrink = jnp.exp2((own_top - top) * POWER)
        mass = jnp.sum(e, 0, keepdims=True) + shrink * stat_ref[g, 1:2]
        inverse = jnp.where(valid, 1.0 / mass, 0.0)
        p = e * inverse
        p_low = p.astype(bf16)
        attended = dot(values, p_low, 0, 0) + own_ref[g] * (shrink * inverse)
        out_ref[g] = unstacked(attended, tokens)
        dp = dot(values, u, 1, 1)
        delta = jnp.sum(u.T.astype(f32) * attended, 0, keepdims=True)
        ds = (p * (dp - delta)).astype(bf16)
        ds_ref[g] = ds
        line_ref[g, 0:1] = jnp.where(valid, top * POWER + jnp.log2(mass), 1e30)
        line_ref[g, 1:2] = delta
        dk = dot(ds, q, 1, 0) * SCALING
        dv = dot(p_low, u, 1, 0)
        for k, ref in enumerate(term_refs):
            ref[:part, cols] = dk[k * part : (k + 1) * part].astype(ref.dtype)
            ref[part:, cols] = dv[k * part : (k + 1) * part].astype(ref.dtype)
        return carry

    lax.fori_loop(0, heads, step, 0)


def rest_kernel(n, group, *refs):
    q_ref, u_ref, ko_ref, vo_ref, att_ref, ds_ref, line_ref, sum_ref, recv_ref, alive_ref = refs[:10]
    pay_refs = refs[10 : 10 + n]
    out_hbm, dq_hbm, dko_hbm, dvo_hbm, weights_ref = refs[10 + n : 15 + n]
    dq_ref, dko_ref, dvo_ref, sems = refs[15 + n :]
    heads, tokens, width = q_ref.shape
    part = (pay_refs[0].shape[0] - EXTRA) // 2

    def early_store(g):
        return pltpu.make_async_copy(att_ref.at[g], out_hbm.at[:, columns_of(g, width)], sems.at[0, g])

    def stores(g):
        slim = columns_of(g, HEAD_SIZE)
        return [
            pltpu.make_async_copy(dq_ref.at[g], dq_hbm.at[:, columns_of(g, width)], sems.at[1, g]),
            pltpu.make_async_copy(dko_ref.at[g], dko_hbm.at[:, slim], sems.at[2, g]),
            pltpu.make_async_copy(dvo_ref.at[g], dvo_hbm.at[:, slim], sems.at[3, g]),
        ]

    for g in range(heads):
        early_store(g).start()
    batch = sum_ref[0:1] + recv_ref[0:1]
    alive = alive_ref[...]
    member = lax.axis_index("resp")
    rewards = [
        jnp.sum(r[2 * part :, :HEAD_SIZE].astype(f32), 0, keepdims=True) for r in pay_refs
    ]
    total = sum(reward * row_of(alive, member ^ k) for k, reward in enumerate(rewards))
    mean = total / jnp.sum(alive, 0, keepdims=True)
    weights = [(reward - mean) / batch for reward in rewards]
    for k in range(n):
        weights_ref[k : k + 1] = weights[k]
    weight = weights[0]
    weight_rows = jnp.concatenate([weight] * (group * tokens // HEAD_SIZE), 1)

    def step(g, carry):
        cols = columns_of(g, HEAD_SIZE)
        keys = jnp.concatenate([r[:part, cols] for r in pay_refs], 0)
        q = stacked(q_ref[g])
        u = stacked(u_ref[g])
        ko, vo = ko_ref[g], vo_ref[g]
        s = dot(ko, q, 1, 1)
        s = jnp.where(causal_mask(tokens, group), s, -1e30)
        p = jnp.exp2(s * POWER - line_ref[g, 0:1])
        dp = dot(vo, u, 1, 1)
        ds = (p * (dp - line_ref[g, 1:2])).astype(bf16)
        dq = dot(keys, ds_ref[g], 0, 0) + dot(ko, ds, 0, 0)
        dq_ref[g] = unstacked(dq * (weight_rows * SCALING), tokens)
        dko_ref[g] = (dot(ds, q, 1, 0) * (weight * SCALING)).astype(bf16)
        dvo_ref[g] = (dot(p.astype(bf16), u, 1, 0) * weight).astype(bf16)
        for copy in stores(g):
            copy.start()
        return carry

    lax.fori_loop(0, heads, step, 0)
    for g in range(heads):
        early_store(g).wait()
        for copy in stores(g):
            copy.wait()


def total_kernel(n, weights_ref, *refs):
    term_refs, (key_ref, value_ref) = refs[:n], refs[n:]
    part, width = key_ref.shape
    total = jnp.zeros((2 * part, width), f32)
    for k, ref in enumerate(term_refs):
        weight = weights_ref[k : k + 1]
        total += ref[...].astype(f32) * jnp.concatenate([weight] * (width // HEAD_SIZE), 1)
    key_ref[...] = total[:part].astype(bf16)
    value_ref[...] = total[part:].astype(bf16)


def local(q, ko, vo, u, kp, vp, kept, spaces, spans, payoffs):
    n = lax.axis_size("resp")
    n_prompt = lax.axis_size("prompt")
    tokens = q.shape[2]
    kv_width = ko.shape[3]
    heads = kv_width // HEAD_SIZE
    group = q.shape[3] // kv_width
    width = group * HEAD_SIZE
    rows = group * tokens
    part = kp.shape[1]
    prefix = n * part
    tile_shape = (8, HEAD_SIZE)
    slots_shape = (-(-n // 8) * 8, HEAD_SIZE)

    vmem = pl.BlockSpec(memory_space=pltpu.VMEM)
    hbm = pl.BlockSpec(memory_space=pl.ANY)
    scalar = pl.BlockSpec(memory_space=pltpu.SMEM)

    def pinned(x):
        return pltpu.with_memory_space_constraint(x, pltpu.HBM)

    def call(kernel, units, ins, out, scratch):
        return pl.pallas_call(
            kernel,
            in_specs=[spec for spec, _ in ins],
            out_specs=[spec for spec, _ in out],
            out_shape=[shape for _, shape in out],
            scratch_shapes=scratch,
            compiler_params=pltpu.CompilerParams(vmem_limit_bytes=VMEM_LIMIT),
            cost_estimate=pl.CostEstimate(
                flops=units * 2 * heads * rows * tokens * HEAD_SIZE,
                bytes_accessed=1 << 20,
                transcendentals=0,
            ),
        )(*[x for _, x in ins])

    def kept_in(shape, kind):
        return (vmem, pltpu.VMEM(shape, kind))

    def given(shape, kind=bf16, spec=hbm):
        return (spec, jax.ShapeDtypeStruct(shape, kind))

    sems = pltpu.SemaphoreType.DMA((4, heads))
    stat = kept_in((heads, 8, rows), f32)
    tile_kind = kept_in(tile_shape, f32)
    slots_kind = kept_in(slots_shape, f32)
    wide, slim = (heads, tokens, width), (heads, tokens, HEAD_SIZE)
    q, ko, vo, u = q[0, 0], ko[0, 0], vo[0, 0], u[0, 0]

    (payload,) = call(
        pack_kernel,
        0,
        [(scalar, payoffs), (hbm, pinned(kp[0])), (hbm, pinned(vp[0]))],
        [kept_in((2 * part + EXTRA, kv_width), bf16)],
        [sems],
    )
    pays = [payload] + [swap(payload, n, k) for k in range(1, n)]

    def across(x, k):
        return lax.ppermute(x, "prompt", [(i, i ^ k) for i in range(n_prompt)])

    small = [kept, spaces, spans, across(kept, 1)]
    q_in, u_in, ko_in, vo_in, own, own_stat, tile, alive = call(
        functools.partial(own_kernel, group, 1),
        2,
        [(hbm, x) for x in small] + [(hbm, pinned(x)) for x in (q, u, ko, vo)],
        [kept_in(wide, bf16)] * 2
        + [kept_in(slim, bf16)] * 2
        + [kept_in((heads, HEAD_SIZE, rows), f32), stat, tile_kind, slots_kind],
        [pltpu.SMEM(x.shape, x.dtype) for x in small]
        + [sems, pltpu.SemaphoreType.DMA((len(small),))],
    )
    k = 2
    while 4 * k < n_prompt:
        tile = tile + across(tile, k)
        k *= 2
    att, ds, line, tile_sum, *terms = call(
        functools.partial(prefix_kernel, n),
        5,
        [(vmem, x) for x in [q_in, u_in, own, own_stat, tile, across(tile, k)] + pays],
        [kept_in(wide, bf16), kept_in((heads, prefix, rows), bf16), stat, tile_kind]
        + [kept_in((2 * part, kv_width), f32 if i == 0 else bf16) for i in range(n)],
        [],
    )
    other = across(tile_sum, 2 * k)
    received = [swap(t, n, i) for i, t in enumerate(terms) if i > 0]
    attn_out, dq, dko, dvo, weights = call(
        functools.partial(rest_kernel, n, group),
        6,
        [(vmem, x) for x in [q_in, u_in, ko_in, vo_in, att, ds, line, tile_sum, other, alive] + pays],
        [given(q.shape), given(q.shape), given(ko.shape), given(ko.shape), slots_kind],
        [pltpu.VMEM(wide, bf16), pltpu.VMEM(slim, bf16), pltpu.VMEM(slim, bf16), sems],
    )
    key_total, value_total = call(
        functools.partial(total_kernel, n),
        0,
        [(vmem, x) for x in [weights, terms[0]] + received],
        [given((part, kv_width), spec=vmem)] * 2,
        [],
    )
    return (
        attn_out[None, None],
        dq[None, None],
        dko[None, None],
        dvo[None, None],
        key_total[None],
        value_total[None],
    )


def solution(mesh):
    wide = P("prompt", "resp", None, None)
    rows = P("prompt", "resp", None)
    pair = P("prompt", "resp")
    return jax.shard_map(
        local,
        mesh=mesh,
        in_specs=(wide, wide, wide, wide, rows, rows, P("prompt"), P("prompt", None), pair, pair),
        out_specs=(wide, wide, wide, wide, rows, rows),
        check_vma=False,
    )
```

```python
import functools
import jax
import jax.numpy as jnp
from jax import lax
from jax.experimental import pallas as pl
from jax.experimental.pallas import tpu as pltpu
from jax.sharding import PartitionSpec as P

HEAD_SIZE = 128
BLOCK = 128
EXTRA = 16
SCALING = HEAD_SIZE**-0.5
POWER = SCALING * 1.4426950408889634
VMEM_LIMIT = 32 << 20
f32 = jnp.float32
bf16 = jnp.bfloat16
i32 = jnp.int32


def dot(a, b, ca, cb):
    return lax.dot_general(a, b, (((ca,), (cb,)), ((), ())), preferred_element_type=f32)


def swap(x, n, k):
    return lax.ppermute(x, "resp", [(i, i ^ k) for i in range(n)])


def columns_of(g, width):
    return pl.ds(pl.multiple_of(g * width, width), width)


def stacked(block):
    width = block.shape[1]
    return jnp.concatenate([block[:, i : i + HEAD_SIZE] for i in range(0, width, HEAD_SIZE)], 0)


def unstacked(x, tokens):
    x = x.astype(bf16)
    return jnp.concatenate([x[:, i : i + tokens].T for i in range(0, x.shape[1], tokens)], 1)


def causal_mask(tokens, group):
    key = lax.broadcasted_iota(i32, (tokens, tokens), 0)
    row = lax.broadcasted_iota(i32, (tokens, tokens), 1)
    return jnp.concatenate([key <= row] * group, 1)


def row_of(tile, index):
    row = lax.broadcasted_iota(i32, tile.shape, 0)
    return jnp.sum(jnp.where(row == index, tile, 0.0), 0, keepdims=True)


def pack_kernel(payoff_ref, kp_hbm, vp_hbm, payload_ref, sems):
    part, width = kp_hbm.shape
    copies = [
        pltpu.make_async_copy(kp_hbm, payload_ref.at[:part], sems.at[0, 0]),
        pltpu.make_async_copy(vp_hbm, payload_ref.at[part : 2 * part], sems.at[1, 0]),
    ]
    for copy in copies:
        copy.start()
    payoff = jnp.full((EXTRA, width), payoff_ref[0, 0], f32)
    high = payoff.astype(bf16).astype(f32)
    middle = (payoff - high).astype(bf16).astype(f32)
    low = payoff - high - middle
    row = lax.broadcasted_iota(i32, payoff.shape, 0)
    pieces = jnp.where(row == 0, high, jnp.where(row == 1, middle, jnp.where(row == 2, low, 0.0)))
    payload_ref[2 * part :] = pieces.astype(bf16)
    for copy in copies:
        copy.wait()


def own_kernel(group, counts, *refs):
    small_hbm, refs = refs[: 3 + counts], refs[3 + counts :]
    q_hbm, u_hbm, ko_hbm, vo_hbm = refs[:4]
    q_ref, u_ref, ko_ref, vo_ref, att_ref, stat_ref, tile_ref, alive_ref = refs[4:12]
    small_refs, sems, small_sems = refs[12:-2], refs[-2], refs[-1]
    heads, tokens, width = q_ref.shape

    def loads(g):
        return [
            pltpu.make_async_copy(ko_hbm.at[:, columns_of(g, HEAD_SIZE)], ko_ref.at[g], sems.at[0, g]),
            pltpu.make_async_copy(q_hbm.at[:, columns_of(g, width)], q_ref.at[g], sems.at[1, g]),
            pltpu.make_async_copy(vo_hbm.at[:, columns_of(g, HEAD_SIZE)], vo_ref.at[g], sems.at[2, g]),
        ]

    def late_load(g):
        return pltpu.make_async_copy(u_hbm.at[:, columns_of(g, width)], u_ref.at[g], sems.at[3, g])

    small = [
        pltpu.make_async_copy(a, b, small_sems.at[i])
        for i, (a, b) in enumerate(zip(small_hbm, small_refs))
    ]
    for copy in small:
        copy.start()
    for g in range(heads):
        for copy in loads(g):
            copy.start()
    for g in range(heads):
        late_load(g).start()

    for copy in small:
        copy.wait()
    kept_ref, spaces_ref, spans_ref = small_refs[:3]
    member = lax.axis_index("resp")
    kept = kept_ref[0]
    row = lax.broadcasted_iota(i32, alive_ref.shape, 0)
    alive = jnp.zeros(alive_ref.shape, f32)
    own_alive = 0
    for i in range(spaces_ref.shape[1]):
        alive += jnp.where((row == spaces_ref[0, i]) & (i < kept), 1.0, 0.0)
        own_alive += jnp.where((spaces_ref[0, i] == member) & (i < kept), 1, 0)
    alive_ref[...] = alive
    count = kept + sum(r[0] for r in small_refs[3:])
    tile_ref[...] = jnp.full(tile_ref.shape, count.astype(f32))
    token = lax.broadcasted_iota(i32, (1, tokens), 1)
    valid = jnp.where(token < own_alive * spans_ref[0, 0] * BLOCK, 1.0, 0.0)
    valid = jnp.concatenate([valid] * group, 1)

    def step(g, carry):
        for copy in loads(g):
            copy.wait()
        s = dot(ko_ref[g], stacked(q_ref[g]), 1, 1)
        s = jnp.where(causal_mask(tokens, group), s, -1e30)
        top = jnp.max(s, 0, keepdims=True)
        e = jnp.exp2((s - top) * POWER)
        stat_ref[g, 0:1] = top
        stat_ref[g, 1:2] = jnp.sum(e, 0, keepdims=True)
        stat_ref[g, 2:3] = valid
        att_ref[g] = dot(vo_ref[g], e.astype(bf16), 0, 0)
        return carry

    lax.fori_loop(0, heads, step, 0)
    for g in range(heads):
        late_load(g).wait()


def prefix_kernel(n, *refs):
    q_ref, u_ref, own_ref, stat_ref = refs[:4]
    pay_refs = refs[4 : 4 + n]
    out_ref, ds_ref, line_ref = refs[4 + n : 7 + n]
    term_refs = refs[7 + n :]
    heads, tokens, width = q_ref.shape
    part = (pay_refs[0].shape[0] - EXTRA) // 2

    def step(g, carry):
        cols = columns_of(g, HEAD_SIZE)
        keys = jnp.concatenate([r[:part, cols] for r in pay_refs], 0)
        values = jnp.concatenate([r[part : 2 * part, cols] for r in pay_refs], 0)
        q = stacked(q_ref[g])
        u = stacked(u_ref[g])
        s = dot(keys, q, 1, 1)
        own_top = stat_ref[g, 0:1]
        valid = stat_ref[g, 2:3] > 0.0
        top = jnp.maximum(jnp.max(s, 0, keepdims=True), own_top)
        e = jnp.exp2((s - top) * POWER)
        shrink = jnp.exp2((own_top - top) * POWER)
        mass = jnp.sum(e, 0, keepdims=True) + shrink * stat_ref[g, 1:2]
        inverse = jnp.where(valid, 1.0 / mass, 0.0)
        p = e * inverse
        p_low = p.astype(bf16)
        attended = dot(values, p_low, 0, 0) + own_ref[g] * (shrink * inverse)
        out_ref[g] = unstacked(attended, tokens)
        dp = dot(values, u, 1, 1)
        delta = jnp.sum(u.T.astype(f32) * attended, 0, keepdims=True)
        ds = (p * (dp - delta)).astype(bf16)
        ds_ref[g] = ds
        line_ref[g, 0:1] = jnp.where(valid, top * POWER + jnp.log2(mass), 1e30)
        line_ref[g, 1:2] = delta
        dk = dot(ds, q, 1, 0) * SCALING
        dv = dot(p_low, u, 1, 0)
        for k, ref in enumerate(term_refs):
            ref[:part, cols] = dk[k * part : (k + 1) * part].astype(ref.dtype)
            ref[part:, cols] = dv[k * part : (k + 1) * part].astype(ref.dtype)
        return carry

    lax.fori_loop(0, heads, step, 0)


def add_kernel(tile_ref, recv_ref, after_ref, sum_ref):
    sum_ref[...] = tile_ref[...] + recv_ref[...]


def rest_kernel(n, group, *refs):
    q_ref, u_ref, ko_ref, vo_ref, att_ref, ds_ref, line_ref, sum_ref, recv_ref, alive_ref = refs[:10]
    pay_refs = refs[10 : 10 + n]
    out_hbm, dq_hbm, dko_hbm, dvo_hbm, weights_ref = refs[10 + n : 15 + n]
    dq_ref, dko_ref, dvo_ref, sems = refs[15 + n :]
    heads, tokens, width = q_ref.shape
    part = (pay_refs[0].shape[0] - EXTRA) // 2

    def early_store(g):
        return pltpu.make_async_copy(att_ref.at[g], out_hbm.at[:, columns_of(g, width)], sems.at[0, g])

    def stores(g):
        slim = columns_of(g, HEAD_SIZE)
        return [
            pltpu.make_async_copy(dq_ref.at[g], dq_hbm.at[:, columns_of(g, width)], sems.at[1, g]),
            pltpu.make_async_copy(dko_ref.at[g], dko_hbm.at[:, slim], sems.at[2, g]),
            pltpu.make_async_copy(dvo_ref.at[g], dvo_hbm.at[:, slim], sems.at[3, g]),
        ]

    for g in range(heads):
        early_store(g).start()
    batch = sum_ref[0:1] + recv_ref[0:1]
    alive = alive_ref[...]
    member = lax.axis_index("resp")
    rewards = [
        jnp.sum(r[2 * part :, :HEAD_SIZE].astype(f32), 0, keepdims=True) for r in pay_refs
    ]
    total = sum(reward * row_of(alive, member ^ k) for k, reward in enumerate(rewards))
    mean = total / jnp.sum(alive, 0, keepdims=True)
    weights = [(reward - mean) / batch for reward in rewards]
    for k in range(n):
        weights_ref[k : k + 1] = weights[k]
    weight = weights[0]
    weight_rows = jnp.concatenate([weight] * (group * tokens // HEAD_SIZE), 1)

    def step(g, carry):
        cols = columns_of(g, HEAD_SIZE)
        keys = jnp.concatenate([r[:part, cols] for r in pay_refs], 0)
        q = stacked(q_ref[g])
        u = stacked(u_ref[g])
        ko, vo = ko_ref[g], vo_ref[g]
        s = dot(ko, q, 1, 1)
        s = jnp.where(causal_mask(tokens, group), s, -1e30)
        p = jnp.exp2(s * POWER - line_ref[g, 0:1])
        dp = dot(vo, u, 1, 1)
        ds = (p * (dp - line_ref[g, 1:2])).astype(bf16)
        dq = dot(keys, ds_ref[g], 0, 0) + dot(ko, ds, 0, 0)
        dq_ref[g] = unstacked(dq * (weight_rows * SCALING), tokens)
        dko_ref[g] = (dot(ds, q, 1, 0) * (weight * SCALING)).astype(bf16)
        dvo_ref[g] = (dot(p.astype(bf16), u, 1, 0) * weight).astype(bf16)
        for copy in stores(g):
            copy.start()
        return carry

    lax.fori_loop(0, heads, step, 0)
    for g in range(heads):
        early_store(g).wait()
        for copy in stores(g):
            copy.wait()


def total_kernel(n, weights_ref, *refs):
    term_refs, (key_ref, value_ref) = refs[:n], refs[n:]
    part, width = key_ref.shape
    total = jnp.zeros((2 * part, width), f32)
    for k, ref in enumerate(term_refs):
        weight = weights_ref[k : k + 1]
        total += ref[...].astype(f32) * jnp.concatenate([weight] * (width // HEAD_SIZE), 1)
    key_ref[...] = total[:part].astype(bf16)
    value_ref[...] = total[part:].astype(bf16)


def local(q, ko, vo, u, kp, vp, kept, spaces, spans, payoffs):
    n = lax.axis_size("resp")
    n_prompt = lax.axis_size("prompt")
    tokens = q.shape[2]
    kv_width = ko.shape[3]
    heads = kv_width // HEAD_SIZE
    group = q.shape[3] // kv_width
    width = group * HEAD_SIZE
    rows = group * tokens
    part = kp.shape[1]
    prefix = n * part
    tile_shape = (8, HEAD_SIZE)
    slots_shape = (-(-n // 8) * 8, HEAD_SIZE)

    vmem = pl.BlockSpec(memory_space=pltpu.VMEM)
    hbm = pl.BlockSpec(memory_space=pl.ANY)
    scalar = pl.BlockSpec(memory_space=pltpu.SMEM)

    def pinned(x):
        return pltpu.with_memory_space_constraint(x, pltpu.HBM)

    def call(kernel, units, ins, out, scratch):
        return pl.pallas_call(
            kernel,
            in_specs=[spec for spec, _ in ins],
            out_specs=[spec for spec, _ in out],
            out_shape=[shape for _, shape in out],
            scratch_shapes=scratch,
            compiler_params=pltpu.CompilerParams(vmem_limit_bytes=VMEM_LIMIT),
            cost_estimate=pl.CostEstimate(
                flops=units * 2 * heads * rows * tokens * HEAD_SIZE,
                bytes_accessed=1 << 20,
                transcendentals=0,
            ),
        )(*[x for _, x in ins])

    def kept_in(shape, kind):
        return (vmem, pltpu.VMEM(shape, kind))

    def given(shape, kind=bf16, spec=hbm):
        return (spec, jax.ShapeDtypeStruct(shape, kind))

    sems = pltpu.SemaphoreType.DMA((4, heads))
    stat = kept_in((heads, 8, rows), f32)
    tile_kind = kept_in(tile_shape, f32)
    slots_kind = kept_in(slots_shape, f32)
    wide, slim = (heads, tokens, width), (heads, tokens, HEAD_SIZE)
    q, ko, vo, u = q[0, 0], ko[0, 0], vo[0, 0], u[0, 0]

    (payload,) = call(
        pack_kernel,
        0,
        [(scalar, payoffs), (hbm, pinned(kp[0])), (hbm, pinned(vp[0]))],
        [kept_in((2 * part + EXTRA, kv_width), bf16)],
        [sems],
    )
    pays = [payload] + [swap(payload, n, k) for k in range(1, n)]

    def across(x, k):
        return lax.ppermute(x, "prompt", [(i, i ^ k) for i in range(n_prompt)])

    small = [kept, pinned(spaces), spans, across(kept, 1)]
    q_in, u_in, ko_in, vo_in, own, own_stat, tile, alive = call(
        functools.partial(own_kernel, group, 1),
        2,
        [(hbm, x) for x in small] + [(hbm, pinned(x)) for x in (q, u, ko, vo)],
        [kept_in(wide, bf16)] * 2
        + [kept_in(slim, bf16)] * 2
        + [kept_in((heads, HEAD_SIZE, rows), f32), stat, tile_kind, slots_kind],
        [pltpu.SMEM(x.shape, x.dtype) for x in small]
        + [sems, pltpu.SemaphoreType.DMA((len(small),))],
    )
    k = 2
    while 4 * k < n_prompt:
        tile = tile + across(tile, k)
        k *= 2
    arriving = across(tile, k)
    att, ds, line, *terms = call(
        functools.partial(prefix_kernel, n),
        5,
        [(vmem, x) for x in [q_in, u_in, own, own_stat] + pays],
        [kept_in(wide, bf16), kept_in((heads, prefix, rows), bf16), stat]
        + [kept_in((2 * part, kv_width), f32 if i == 0 else bf16) for i in range(n)],
        [],
    )
    (tile_sum,) = call(
        add_kernel, 0, [(vmem, tile), (vmem, arriving), (hbm, line)], [tile_kind], []
    )
    other = across(tile_sum, 2 * k)
    received = [swap(t, n, i) for i, t in enumerate(terms) if i > 0]
    attn_out, dq, dko, dvo, weights = call(
        functools.partial(rest_kernel, n, group),
        6,
        [(vmem, x) for x in [q_in, u_in, ko_in, vo_in, att, ds, line, tile_sum, other, alive] + pays],
        [given(q.shape), given(q.shape), given(ko.shape), given(ko.shape), slots_kind],
        [pltpu.VMEM(wide, bf16), pltpu.VMEM(slim, bf16), pltpu.VMEM(slim, bf16), sems],
    )
    key_total, value_total = call(
        functools.partial(total_kernel, n),
        0,
        [(vmem, x) for x in [weights, terms[0]] + received],
        [given((part, kv_width), spec=vmem)] * 2,
        [],
    )
    return (
        attn_out[None, None],
        dq[None, None],
        dko[None, None],
        dvo[None, None],
        key_total[None],
        value_total[None],
    )


def solution(mesh):
    wide = P("prompt", "resp", None, None)
    rows = P("prompt", "resp", None)
    pair = P("prompt", "resp")
    return jax.shard_map(
        local,
        mesh=mesh,
        in_specs=(wide, wide, wide, wide, rows, rows, P("prompt"), P("prompt", None), pair, pair),
        out_specs=(wide, wide, wide, wide, rows, rows),
        check_vma=False,
    )
```

```python
import functools
import jax
import jax.numpy as jnp
from jax import lax
from jax.experimental import pallas as pl
from jax.experimental.pallas import tpu as pltpu
from jax.sharding import PartitionSpec as P

HEAD_SIZE = 128
BLOCK = 128
EXTRA = 16
SCALING = HEAD_SIZE**-0.5
POWER = SCALING * 1.4426950408889634
VMEM_LIMIT = 32 << 20
f32 = jnp.float32
bf16 = jnp.bfloat16
i32 = jnp.int32


def dot(a, b, ca, cb):
    return lax.dot_general(a, b, (((ca,), (cb,)), ((), ())), preferred_element_type=f32)


def swap(x, n, k):
    return lax.ppermute(x, "resp", [(i, i ^ k) for i in range(n)])


def columns_of(g, width):
    return pl.ds(pl.multiple_of(g * width, width), width)


def stacked(block):
    width = block.shape[1]
    return jnp.concatenate([block[:, i : i + HEAD_SIZE] for i in range(0, width, HEAD_SIZE)], 0)


def unstacked(x, tokens):
    x = x.astype(bf16)
    return jnp.concatenate([x[i : i + tokens] for i in range(0, x.shape[0], tokens)], 1)


def spread(x, width):
    return jnp.concatenate([x] * (width // HEAD_SIZE), 1)


def with_ones(values):
    return jnp.concatenate([values, jnp.ones(values.shape, bf16)], 1)


def causal_mask(tokens, group):
    row = lax.broadcasted_iota(i32, (tokens, tokens), 0)
    key = lax.broadcasted_iota(i32, (tokens, tokens), 1)
    return jnp.concatenate([key <= row] * group, 0)


def row_of(tile, index):
    row = lax.broadcasted_iota(i32, tile.shape, 0)
    return jnp.sum(jnp.where(row == index, tile, 0.0), 0, keepdims=True)


def pack_kernel(payoff_ref, kp_hbm, vp_hbm, payload_ref, sems):
    part, width = kp_hbm.shape
    copies = [
        pltpu.make_async_copy(kp_hbm, payload_ref.at[:part], sems.at[0, 0]),
        pltpu.make_async_copy(vp_hbm, payload_ref.at[part : 2 * part], sems.at[1, 0]),
    ]
    for copy in copies:
        copy.start()
    payoff = jnp.full((EXTRA, width), payoff_ref[0, 0], f32)
    high = payoff.astype(bf16).astype(f32)
    middle = (payoff - high).astype(bf16).astype(f32)
    low = payoff - high - middle
    row = lax.broadcasted_iota(i32, payoff.shape, 0)
    pieces = jnp.where(row == 0, high, jnp.where(row == 1, middle, jnp.where(row == 2, low, 0.0)))
    payload_ref[2 * part :] = pieces.astype(bf16)
    for copy in copies:
        copy.wait()


def own_kernel(group, counts, *refs):
    small_hbm, refs = refs[: 3 + counts], refs[3 + counts :]
    q_hbm, u_hbm, ko_hbm, vo_hbm = refs[:4]
    q_ref, u_ref, ko_ref, vo_ref, att_ref, lse_ref, tile_ref, alive_ref, length_ref = refs[4:13]
    small_refs, sems, small_sems = refs[13:-2], refs[-2], refs[-1]
    heads, tokens, width = q_ref.shape

    def loads(g):
        return [
            pltpu.make_async_copy(ko_hbm.at[:, columns_of(g, HEAD_SIZE)], ko_ref.at[g], sems.at[0, g]),
            pltpu.make_async_copy(q_hbm.at[:, columns_of(g, width)], q_ref.at[g], sems.at[1, g]),
            pltpu.make_async_copy(vo_hbm.at[:, columns_of(g, HEAD_SIZE)], vo_ref.at[g], sems.at[2, g]),
        ]

    def late_load(g):
        return pltpu.make_async_copy(u_hbm.at[:, columns_of(g, width)], u_ref.at[g], sems.at[3, g])

    small = [
        pltpu.make_async_copy(a, b, small_sems.at[i])
        for i, (a, b) in enumerate(zip(small_hbm, small_refs))
    ]
    for copy in small:
        copy.start()
    for g in range(heads):
        for copy in loads(g):
            copy.start()
    for g in range(heads):
        late_load(g).start()

    for copy in small:
        copy.wait()
    kept_ref, spaces_ref, spans_ref = small_refs[:3]
    member = lax.axis_index("resp")
    kept = kept_ref[0]
    row = lax.broadcasted_iota(i32, alive_ref.shape, 0)
    alive = jnp.zeros(alive_ref.shape, f32)
    own_alive = 0
    for i in range(spaces_ref.shape[1]):
        alive += jnp.where((row == spaces_ref[0, i]) & (i < kept), 1.0, 0.0)
        own_alive += jnp.where((spaces_ref[0, i] == member) & (i < kept), 1, 0)
    alive_ref[...] = alive
    count = kept + sum(r[0] for r in small_refs[3:])
    tile_ref[...] = jnp.full(tile_ref.shape, count.astype(f32))
    length = own_alive * spans_ref[0, 0] * BLOCK
    length_ref[...] = jnp.full(length_ref.shape, length.astype(f32))

    for g in range(heads):
        for copy in loads(g):
            copy.wait()

    def step(g, carry):
        s = dot(stacked(q_ref[g]), ko_ref[g], 1, 1)
        s = jnp.where(causal_mask(tokens, group), s, -1e30)
        top = jnp.max(s, 1, keepdims=True) * POWER
        e = jnp.exp2(s * POWER - top)
        both = dot(e.astype(bf16), with_ones(vo_ref[g]), 1, 0)
        mass = both[:, HEAD_SIZE:]
        att_ref[g] = both[:, :HEAD_SIZE] / mass
        lse_ref[g] = jnp.log2(mass) + top
        return carry

    lax.fori_loop(0, heads, step, 0, unroll=True)
    for g in range(heads):
        late_load(g).wait()


def prefix_kernel(n, *refs):
    q_ref, u_ref, own_ref, lse_ref, length_ref = refs[:5]
    pay_refs = refs[5 : 5 + n]
    out_ref, grad_ref, ds_ref, top_ref, delta_ref = refs[5 + n : 10 + n]
    term_refs = refs[10 + n :]
    heads, tokens, width = q_ref.shape
    group = width // HEAD_SIZE
    part = (pay_refs[0].shape[0] - EXTRA) // 2
    token = lax.broadcasted_iota(i32, (tokens, HEAD_SIZE), 0).astype(f32)
    valid = jnp.concatenate([token < length_ref[0:1]] * group, 0)

    def step(g, carry):
        cols = columns_of(g, HEAD_SIZE)
        keys = jnp.concatenate([r[:part, cols] for r in pay_refs], 0)
        values = jnp.concatenate([r[part : 2 * part, cols] for r in pay_refs], 0)
        q = stacked(q_ref[g])
        s = dot(q, keys, 1, 1)
        own_lse = lse_ref[g]
        top = jnp.maximum(jnp.max(s, 1, keepdims=True) * POWER, own_lse)
        e = jnp.exp2(s * POWER - spread(top, s.shape[1]))
        e_low = e.astype(bf16)
        both = dot(e_low, with_ones(values), 1, 0)
        own_mass = jnp.exp2(own_lse - top)
        inverse = jnp.where(valid, 1.0 / (both[:, HEAD_SIZE:] + own_mass), 0.0)
        attended = (both[:, :HEAD_SIZE] + own_ref[g] * own_mass) * inverse
        out_ref[g] = unstacked(attended, tokens)
        grad = (stacked(u_ref[g]).astype(f32) * inverse).astype(bf16)
        grad_ref[g] = grad
        dp = dot(grad, values, 1, 1)
        delta = jnp.sum(grad.astype(f32) * attended, 1, keepdims=True)
        ds = (e * (dp - delta)).astype(bf16)
        ds_ref[g] = ds
        top_ref[g] = top
        delta_ref[g] = jnp.broadcast_to(delta, top.shape)
        dk = dot(q, ds, 0, 0).T * SCALING
        dv = dot(grad, e_low, 0, 0).T
        for k, ref in enumerate(term_refs):
            ref[:part, cols] = dk[k * part : (k + 1) * part].astype(ref.dtype)
            ref[part : 2 * part, cols] = dv[k * part : (k + 1) * part].astype(ref.dtype)
        return carry

    lax.fori_loop(0, heads, step, 0, unroll=True)


def add_kernel(tile_ref, recv_ref, after_ref, sum_ref):
    sum_ref[...] = tile_ref[...] + recv_ref[...]


def rest_kernel(n, group, *refs):
    q_ref, grad_ref, ko_ref, vo_ref, att_ref, ds_ref, top_ref, delta_ref = refs[:8]
    sum_ref, recv_ref, alive_ref = refs[8:11]
    pay_refs = refs[11 : 11 + n]
    out_hbm, dq_hbm, dko_hbm, dvo_hbm, weights_ref = refs[11 + n : 16 + n]
    dq_ref, dko_ref, dvo_ref, sems = refs[16 + n :]
    heads, tokens, width = q_ref.shape
    part = (pay_refs[0].shape[0] - EXTRA) // 2

    def early_store(g):
        return pltpu.make_async_copy(att_ref.at[g], out_hbm.at[:, columns_of(g, width)], sems.at[0, g])

    def stores(g):
        slim = columns_of(g, HEAD_SIZE)
        return [
            pltpu.make_async_copy(dq_ref.at[g], dq_hbm.at[:, columns_of(g, width)], sems.at[1, g]),
            pltpu.make_async_copy(dko_ref.at[g], dko_hbm.at[:, slim], sems.at[2, g]),
            pltpu.make_async_copy(dvo_ref.at[g], dvo_hbm.at[:, slim], sems.at[3, g]),
        ]

    for g in range(heads):
        early_store(g).start()
    batch = sum_ref[0:1] + recv_ref[0:1]
    alive = alive_ref[...]
    member = lax.axis_index("resp")
    rewards = [
        jnp.sum(r[2 * part :, :HEAD_SIZE].astype(f32), 0, keepdims=True) for r in pay_refs
    ]
    total = sum(reward * row_of(alive, member ^ k) for k, reward in enumerate(rewards))
    mean = total / jnp.sum(alive, 0, keepdims=True)
    weights = [(reward - mean) / batch for reward in rewards]
    for k in range(n):
        weights_ref[k : k + 1] = weights[k]
    weight = weights[0]

    def step(g, carry):
        cols = columns_of(g, HEAD_SIZE)
        keys = jnp.concatenate([r[:part, cols] for r in pay_refs], 0)
        q = stacked(q_ref[g])
        ko, vo = ko_ref[g], vo_ref[g]
        grad = grad_ref[g]
        s = dot(q, ko, 1, 1) * POWER - spread(top_ref[g], tokens)
        e = jnp.exp2(jnp.where(causal_mask(tokens, group), s, -1e30))
        dp = dot(grad, vo, 1, 1)
        ds = (e * (dp - spread(delta_ref[g], tokens))).astype(bf16)
        all_ds = jnp.concatenate([ds_ref[g], ds], 1)
        dq = dot(all_ds, jnp.concatenate([keys, ko], 0), 1, 0)
        dq_ref[g] = unstacked(dq * (weight * SCALING), tokens)
        dko_ref[g] = (dot(q, ds, 0, 0).T * (weight * SCALING)).astype(bf16)
        dvo_ref[g] = (dot(grad, e.astype(bf16), 0, 0).T * weight).astype(bf16)
        for copy in stores(g):
            copy.start()
        return carry

    lax.fori_loop(0, heads, step, 0, unroll=True)
    for g in range(heads):
        early_store(g).wait()
        for copy in stores(g):
            copy.wait()


def total_kernel(n, weights_ref, *refs):
    term_refs, (key_ref, value_ref) = refs[:n], refs[n:]
    part, width = key_ref.shape
    total = jnp.zeros((2 * part, width), f32)
    for k, ref in enumerate(term_refs):
        weight = weights_ref[k : k + 1]
        total += ref[...].astype(f32) * jnp.concatenate([weight] * (width // HEAD_SIZE), 1)
    key_ref[...] = total[:part].astype(bf16)
    value_ref[...] = total[part:].astype(bf16)


def local(q, ko, vo, u, kp, vp, kept, spaces, spans, payoffs):
    n = lax.axis_size("resp")
    n_prompt = lax.axis_size("prompt")
    tokens = q.shape[2]
    kv_width = ko.shape[3]
    heads = kv_width // HEAD_SIZE
    group = q.shape[3] // kv_width
    width = group * HEAD_SIZE
    rows = group * tokens
    part = kp.shape[1]
    prefix = n * part
    tile_shape = (8, HEAD_SIZE)
    slots_shape = (-(-n // 8) * 8, HEAD_SIZE)

    vmem = pl.BlockSpec(memory_space=pltpu.VMEM)
    hbm = pl.BlockSpec(memory_space=pl.ANY)
    scalar = pl.BlockSpec(memory_space=pltpu.SMEM)

    def pinned(x):
        return pltpu.with_memory_space_constraint(x, pltpu.HBM)

    def call(kernel, units, ins, out, scratch):
        return pl.pallas_call(
            kernel,
            in_specs=[spec for spec, _ in ins],
            out_specs=[spec for spec, _ in out],
            out_shape=[shape for _, shape in out],
            scratch_shapes=scratch,
            compiler_params=pltpu.CompilerParams(vmem_limit_bytes=VMEM_LIMIT),
            cost_estimate=pl.CostEstimate(
                flops=units * 2 * heads * rows * tokens * HEAD_SIZE,
                bytes_accessed=1 << 20,
                transcendentals=0,
            ),
        )(*[x for _, x in ins])

    def kept_in(shape, kind):
        return (vmem, pltpu.VMEM(shape, kind))

    def given(shape, kind=bf16, spec=hbm):
        return (spec, jax.ShapeDtypeStruct(shape, kind))

    sems = pltpu.SemaphoreType.DMA((4, heads))
    stat = kept_in((heads, rows, HEAD_SIZE), f32)
    tile_kind = kept_in(tile_shape, f32)
    slots_kind = kept_in(slots_shape, f32)
    wide, slim = (heads, tokens, width), (heads, tokens, HEAD_SIZE)
    q, ko, vo, u = q[0, 0], ko[0, 0], vo[0, 0], u[0, 0]

    (payload,) = call(
        pack_kernel,
        0,
        [(scalar, payoffs), (hbm, pinned(kp[0])), (hbm, pinned(vp[0]))],
        [kept_in((2 * part + EXTRA, kv_width), bf16)],
        [sems],
    )
    pays = [payload] + [swap(payload, n, k) for k in range(1, n)]

    def across(x, k):
        return lax.ppermute(x, "prompt", [(i, i ^ k) for i in range(n_prompt)])

    small = [kept, pinned(spaces), spans, across(kept, 1)]
    q_in, u_in, ko_in, vo_in, own, own_lse, tile, alive, length = call(
        functools.partial(own_kernel, group, 1),
        2,
        [(hbm, x) for x in small] + [(hbm, pinned(x)) for x in (q, u, ko, vo)],
        [kept_in(wide, bf16)] * 2
        + [kept_in(slim, bf16)] * 2
        + [stat, stat, tile_kind, slots_kind, tile_kind],
        [pltpu.SMEM(x.shape, x.dtype) for x in small]
        + [sems, pltpu.SemaphoreType.DMA((len(small),))],
    )
    k = 2
    while 4 * k < n_prompt:
        tile = tile + across(tile, k)
        k *= 2
    arriving = across(tile, k)
    att, grad, ds, top, delta, *terms = call(
        functools.partial(prefix_kernel, n),
        5,
        [(vmem, x) for x in [q_in, u_in, own, own_lse, length] + pays],
        [kept_in(wide, bf16), kept_in((heads, rows, HEAD_SIZE), bf16)]
        + [kept_in((heads, rows, prefix), bf16), stat, stat]
        + [kept_in((2 * part, kv_width), f32 if i == 0 else bf16) for i in range(n)],
        [],
    )
    (tile_sum,) = call(
        add_kernel, 0, [(vmem, tile), (vmem, arriving), (hbm, top)], [tile_kind], []
    )
    other = across(tile_sum, 2 * k)
    received = [swap(t, n, i) for i, t in enumerate(terms) if i > 0]
    attn_out, dq, dko, dvo, weights = call(
        functools.partial(rest_kernel, n, group),
        6,
        [(vmem, x) for x in [q_in, grad, ko_in, vo_in, att, ds, top, delta, tile_sum, other, alive] + pays],
        [given(q.shape), given(q.shape), given(ko.shape), given(ko.shape), slots_kind],
        [pltpu.VMEM(wide, bf16), pltpu.VMEM(slim, bf16), pltpu.VMEM(slim, bf16), sems],
    )
    key_total, value_total = call(
        functools.partial(total_kernel, n),
        0,
        [(vmem, x) for x in [weights, terms[0]] + received],
        [given((part, kv_width), spec=vmem)] * 2,
        [],
    )
    return (
        attn_out[None, None],
        dq[None, None],
        dko[None, None],
        dvo[None, None],
        key_total[None],
        value_total[None],
    )


def solution(mesh):
    wide = P("prompt", "resp", None, None)
    rows = P("prompt", "resp", None)
    pair = P("prompt", "resp")
    return jax.shard_map(
        local,
        mesh=mesh,
        in_specs=(wide, wide, wide, wide, rows, rows, P("prompt"), P("prompt", None), pair, pair),
        out_specs=(wide, wide, wide, wide, rows, rows),
        check_vma=False,
    )
```

```python
import functools
import jax
import jax.numpy as jnp
from jax import lax
from jax.experimental import pallas as pl
from jax.experimental.pallas import tpu as pltpu
from jax.sharding import PartitionSpec as P

HEAD_SIZE = 128
BLOCK = 128
EXTRA = 16
SCALING = HEAD_SIZE**-0.5
POWER = SCALING * 1.4426950408889634
VMEM_LIMIT = 32 << 20
f32 = jnp.float32
bf16 = jnp.bfloat16
i32 = jnp.int32


def dot(a, b, ca, cb):
    return lax.dot_general(a, b, (((ca,), (cb,)), ((), ())), preferred_element_type=f32)


def swap(x, n, k):
    return lax.ppermute(x, "resp", [(i, i ^ k) for i in range(n)])


def columns_of(g, width):
    return pl.ds(pl.multiple_of(g * width, width), width)


def stacked(block):
    tokens, width = block.shape
    return jnp.concatenate(
        [
            block[t : t + BLOCK, i : i + HEAD_SIZE]
            for t in range(0, tokens, BLOCK)
            for i in range(0, width, HEAD_SIZE)
        ],
        0,
    )


def unstacked(x, group):
    x = x.astype(bf16)
    lines = [
        jnp.concatenate([x[t + i * BLOCK : t + (i + 1) * BLOCK] for i in range(group)], 1)
        for t in range(0, x.shape[0], group * BLOCK)
    ]
    return jnp.concatenate(lines, 0)


def row_blocks(rows, group):
    return [(slice(t, t + group * BLOCK), t // group + BLOCK) for t in range(0, rows, group * BLOCK)]


def spread(x, width):
    return jnp.concatenate([x] * (width // HEAD_SIZE), 1)


def with_ones(values):
    return jnp.concatenate([values, jnp.ones(values.shape, bf16)], 1)


def causal_mask(group):
    row = lax.broadcasted_iota(i32, (BLOCK, BLOCK), 0)
    key = lax.broadcasted_iota(i32, (BLOCK, BLOCK), 1)
    return jnp.concatenate([key <= row] * group, 0)


def row_of(tile, index):
    row = lax.broadcasted_iota(i32, tile.shape, 0)
    return jnp.sum(jnp.where(row == index, tile, 0.0), 0, keepdims=True)


def pack_kernel(kp_hbm, vp_hbm, ko_hbm, vo_hbm, q_hbm, payload_ref, ko_ref, vo_ref, q_ref, sems):
    part = kp_hbm.shape[0]
    heads, width = ko_ref.shape[0], q_ref.shape[1]
    copies = [
        pltpu.make_async_copy(kp_hbm, payload_ref.at[:part], sems.at[0, 0]),
        pltpu.make_async_copy(vp_hbm, payload_ref.at[part:], sems.at[1, 0]),
        pltpu.make_async_copy(q_hbm.at[:, :width], q_ref, sems.at[2, 0]),
    ]
    for g in range(heads):
        cols = columns_of(g, HEAD_SIZE)
        copies.append(pltpu.make_async_copy(ko_hbm.at[:, cols], ko_ref.at[g], sems.at[3, g]))
        copies.append(pltpu.make_async_copy(vo_hbm.at[:, cols], vo_ref.at[g], sems.at[4, g]))
    for copy in copies:
        copy.start()
    for copy in copies:
        copy.wait()


def reward_rows(payoff):
    whole = jnp.full((EXTRA, HEAD_SIZE), payoff, f32)
    high = whole.astype(bf16).astype(f32)
    middle = (whole - high).astype(bf16).astype(f32)
    low = whole - high - middle
    row = lax.broadcasted_iota(i32, whole.shape, 0)
    return jnp.where(row == 0, high, jnp.where(row == 1, middle, jnp.where(row == 2, low, 0.0)))


def own_kernel(group, counts, *refs):
    small_hbm, refs = refs[: 4 + counts], refs[4 + counts :]
    q_hbm, u_hbm, q_first, ko_ref, vo_ref = refs[:5]
    q_ref, u_ref, att_ref, lse_ref, tile_ref, alive_ref, length_ref = refs[5:12]
    qt_ref, ut_ref, s_ref, reward_ref = refs[12:16]
    small_refs, sems, small_sems = refs[16:-2], refs[-2], refs[-1]
    heads, tokens, width = q_ref.shape

    def load(g):
        return pltpu.make_async_copy(q_hbm.at[:, columns_of(g, width)], q_ref.at[g], sems.at[0, g])

    def late_load(g):
        return pltpu.make_async_copy(u_hbm.at[:, columns_of(g, width)], u_ref.at[g], sems.at[1, g])

    small = [
        pltpu.make_async_copy(a, b, small_sems.at[i])
        for i, (a, b) in enumerate(zip(small_hbm, small_refs))
    ]
    for copy in small:
        copy.start()
    for g in range(1, heads):
        load(g).start()
    for g in range(heads):
        late_load(g).start()

    mask = causal_mask(group)

    def step(g, carry):
        q, ko, vo = stacked(q_ref[g]), ko_ref[g], vo_ref[g]
        for at, span in row_blocks(q.shape[0], group):
            s = dot(q[at], ko[:span], 1, 1) * POWER
            open_part = [s[:, : span - BLOCK]] if span > BLOCK else []
            s = jnp.concatenate(open_part + [jnp.where(mask, s[:, span - BLOCK :], -1e30)], 1)
            s_ref[g, at, :span] = s
            top = jnp.max(s, 1, keepdims=True)
            e = jnp.exp2(s - top)
            both = dot(e.astype(bf16), with_ones(vo[:span]), 1, 0)
            mass = both[:, HEAD_SIZE:]
            att_ref[g, at] = both[:, :HEAD_SIZE] / mass
            lse_ref[g, at] = jnp.log2(mass) + top
        qt_ref[g] = q.T
        return carry

    q_ref[0] = q_first[...]
    step(0, 0)
    for copy in small:
        copy.wait()
    kept_ref, spaces_ref, spans_ref, payoff_ref = small_refs[:4]
    reward_ref[...] = reward_rows(payoff_ref[0, 0])
    member = lax.axis_index("resp")
    kept = kept_ref[0]
    row = lax.broadcasted_iota(i32, alive_ref.shape, 0)
    alive = jnp.zeros(alive_ref.shape, f32)
    own_alive = 0
    for i in range(spaces_ref.shape[1]):
        alive += jnp.where((row == spaces_ref[0, i]) & (i < kept), 1.0, 0.0)
        own_alive += jnp.where((spaces_ref[0, i] == member) & (i < kept), 1, 0)
    alive_ref[...] = alive
    count = kept + sum(r[0] for r in small_refs[4:])
    tile_ref[...] = jnp.full(tile_ref.shape, count.astype(f32))
    length = own_alive * spans_ref[0, 0] * BLOCK
    length_ref[...] = jnp.full(length_ref.shape, length.astype(f32))

    for g in range(1, heads):
        load(g).wait()
    lax.fori_loop(1, heads, step, 0, unroll=True)
    for g in range(heads):
        late_load(g).wait()
    for g in range(heads):
        ut_ref[g] = stacked(u_ref[g]).T


def prefix_kernel(n, *refs):
    q_ref, u_ref, own_ref, lse_ref, length_ref, qt_ref, ut_ref, reward_ref = refs[:8]
    pay_refs = refs[8 : 8 + n]
    out_ref, ds_ref, line_ref, delta_ref = refs[8 + n : 12 + n]
    term_refs = refs[12 + n :]
    for ref in term_refs:
        ref[-EXTRA:] = reward_ref[...].astype(ref.dtype)
    heads, tokens, width = q_ref.shape
    group = width // HEAD_SIZE
    part = pay_refs[0].shape[0] // 2
    token = lax.broadcasted_iota(i32, (tokens, HEAD_SIZE), 0).astype(f32)
    fits = token < length_ref[0:1]
    valid = jnp.concatenate(
        [fits[t : t + BLOCK] for t in range(0, tokens, BLOCK) for _ in range(group)], 0
    )

    def step(g, carry):
        cols = columns_of(g, HEAD_SIZE)
        keys = jnp.concatenate([r[:part, cols] for r in pay_refs], 0)
        values = jnp.concatenate([r[part : 2 * part, cols] for r in pay_refs], 0)
        q = stacked(q_ref[g])
        s = dot(q, keys, 1, 1)
        own_lse = lse_ref[g]
        top = jnp.maximum(jnp.max(s, 1, keepdims=True) * POWER, own_lse)
        e = jnp.exp2(s * POWER - spread(top, s.shape[1]))
        both = dot(e.astype(bf16), with_ones(values), 1, 0)
        own_mass = jnp.exp2(own_lse - top)
        mass = both[:, HEAD_SIZE:] + own_mass
        inverse = jnp.where(valid, 1.0 / mass, 0.0)
        attended = (both[:, :HEAD_SIZE] + own_ref[g] * own_mass) * inverse
        out_ref[g] = unstacked(attended, group)
        p = e * spread(inverse, s.shape[1])
        u = stacked(u_ref[g])
        dp = dot(u, values, 1, 1)
        delta = jnp.sum(u.astype(f32) * attended, 1, keepdims=True)
        ds = (p * (dp - delta)).astype(bf16)
        ds_ref[g] = ds
        line_ref[g] = jnp.where(valid, top + jnp.log2(mass), 1e30)
        delta_ref[g] = jnp.broadcast_to(delta, top.shape)
        dk = dot(qt_ref[g], ds, 1, 0).T * SCALING
        dv = dot(ut_ref[g], p.astype(bf16), 1, 0).T
        for k, ref in enumerate(term_refs):
            at = 2 * g * part
            ref[pl.ds(at, part)] = dk[k * part : (k + 1) * part].astype(ref.dtype)
            ref[pl.ds(at + part, part)] = dv[k * part : (k + 1) * part].astype(ref.dtype)
        return carry

    lax.fori_loop(0, heads, step, 0, unroll=True)


def add_kernel(tile_ref, recv_ref, after_ref, sum_ref):
    sum_ref[...] = tile_ref[...] + recv_ref[...]


def rest_kernel(n, group, begin, end, *refs):
    u_ref, ko_ref, vo_ref, att_ref, ds_ref, line_ref, delta_ref = refs[:7]
    qt_ref, ut_ref, s_ref = refs[7:10]
    pay_refs = refs[10 : 10 + n]
    dq_ref, dko_ref, dvo_ref = refs[10 + n : 13 + n]
    out_hbm, sems = refs[13 + n :] if len(refs) > 13 + n else (None, None)
    _, tokens, width = u_ref.shape
    part = pay_refs[0].shape[0] // 2

    def store(g):
        return pltpu.make_async_copy(att_ref.at[g], out_hbm.at[:, columns_of(g, width)], sems.at[0, g])

    stored = range(u_ref.shape[0]) if out_hbm is not None else ()
    for g in stored:
        store(g).start()

    def step(g, carry):
        cols = columns_of(g, HEAD_SIZE)
        keys = jnp.concatenate([r[:part, cols] for r in pay_refs], 0)
        u, ko, vo = stacked(u_ref[g]), ko_ref[g], vo_ref[g]
        dk, dv = 0.0, 0.0
        for at, span in row_blocks(u.shape[0], group):
            p = jnp.exp2(s_ref[g, at, :span] - spread(line_ref[g, at], span))
            dp = dot(u[at], vo[:span], 1, 1)
            ds = (p * (dp - spread(delta_ref[g, at], span))).astype(bf16)
            all_ds = jnp.concatenate([ds_ref[g, at], ds], 1)
            dq_ref[g - begin, at] = dot(all_ds, jnp.concatenate([keys, ko[:span]], 0), 1, 0)
            missing = [jnp.zeros((HEAD_SIZE, tokens - span), f32)] if span < tokens else []
            dk += jnp.concatenate([dot(qt_ref[g, :, at], ds, 1, 0)] + missing, 1)
            dv += jnp.concatenate([dot(ut_ref[g, :, at], p.astype(bf16), 1, 0)] + missing, 1)
        dko_ref[g - begin] = dk.T
        dvo_ref[g - begin] = dv.T
        return carry

    lax.fori_loop(begin, end, step, 0, unroll=True)
    for g in stored:
        store(g).wait()


def total_kernel(order, alive_ref, *refs):
    term_refs, (total_ref, weight_ref) = refs[:-2], refs[-2:]
    alive = alive_ref[...]
    member = lax.axis_index("resp")
    rewards = [jnp.sum(r[-EXTRA:].astype(f32), 0, keepdims=True) for r in term_refs]
    total = sum(reward * row_of(alive, member ^ k) for k, reward in zip(order, rewards))
    mean = total / jnp.sum(alive, 0, keepdims=True)
    weights = [reward - mean for reward in rewards]
    rows = total_ref.shape[0]
    total_ref[...] = sum(r[:rows].astype(f32) * w for r, w in zip(term_refs, weights))
    weight_ref[...] = jnp.broadcast_to(weights[0], weight_ref.shape)


def last_kernel(group, *refs):
    dq_ref, dko_ref, dvo_ref, sum_ref, total_ref, weight_ref, recv_ref = refs[:7]
    dq_hbm, dko_hbm, dvo_hbm, key_hbm, value_hbm = refs[7:12]
    dq_low, dko_low, dvo_low, key_ref, value_ref, sems = refs[12:]
    heads = dko_low.shape[0]
    part = key_ref.shape[0]
    width = group * HEAD_SIZE

    def stores(g):
        wide, slim = columns_of(g, width), columns_of(g, HEAD_SIZE)
        return [
            pltpu.make_async_copy(dq_low.at[g], dq_hbm.at[:, wide], sems.at[0, g]),
            pltpu.make_async_copy(dko_low.at[g], dko_hbm.at[:, slim], sems.at[1, g]),
            pltpu.make_async_copy(dvo_low.at[g], dvo_hbm.at[:, slim], sems.at[2, g]),
        ]

    totals = [
        pltpu.make_async_copy(key_ref, key_hbm, sems.at[3, 0]),
        pltpu.make_async_copy(value_ref, value_hbm, sems.at[3, 1]),
    ]
    share = 1.0 / (sum_ref[0:1] + recv_ref[0:1])
    weight = weight_ref[0:1] * share
    for g in range(heads):
        dq_low[g] = unstacked(dq_ref[g] * (weight * SCALING), group)
        dko_low[g] = (dko_ref[g] * (weight * SCALING)).astype(bf16)
        dvo_low[g] = (dvo_ref[g] * weight).astype(bf16)
        for copy in stores(g):
            copy.start()
    for g in range(heads):
        for at, ref in ((2 * g * part, key_ref), ((2 * g + 1) * part, value_ref)):
            whole = (total_ref[at : at + part] * share).astype(bf16)
            ref[:, g * HEAD_SIZE : (g + 1) * HEAD_SIZE] = whole
    for copy in totals:
        copy.start()
    for g in range(heads):
        for copy in stores(g):
            copy.wait()
    for copy in totals:
        copy.wait()


def local(q, ko, vo, u, kp, vp, kept, spaces, spans, payoffs):
    n = lax.axis_size("resp")
    n_prompt = lax.axis_size("prompt")
    tokens = q.shape[2]
    kv_width = ko.shape[3]
    heads = kv_width // HEAD_SIZE
    group = q.shape[3] // kv_width
    width = group * HEAD_SIZE
    rows = group * tokens
    part = kp.shape[1]
    prefix = n * part
    tile_shape = (8, HEAD_SIZE)
    slots_shape = (-(-n // 8) * 8, HEAD_SIZE)

    vmem = pl.BlockSpec(memory_space=pltpu.VMEM)
    hbm = pl.BlockSpec(memory_space=pl.ANY)

    def pinned(x):
        return pltpu.with_memory_space_constraint(x, pltpu.HBM)

    def call(kernel, units, ins, out, scratch):
        return pl.pallas_call(
            kernel,
            in_specs=[spec for spec, _ in ins],
            out_specs=[spec for spec, _ in out],
            out_shape=[shape for _, shape in out],
            scratch_shapes=scratch,
            compiler_params=pltpu.CompilerParams(vmem_limit_bytes=VMEM_LIMIT),
            cost_estimate=pl.CostEstimate(
                flops=units * 2 * heads * rows * tokens * HEAD_SIZE,
                bytes_accessed=1 << 20,
                transcendentals=0,
            ),
        )(*[x for _, x in ins])

    def kept_in(shape, kind):
        return (vmem, pltpu.VMEM(shape, kind))

    def given(shape, kind=bf16, spec=hbm):
        return (spec, jax.ShapeDtypeStruct(shape, kind))

    sems = pltpu.SemaphoreType.DMA((5, heads))
    stat = kept_in((heads, rows, HEAD_SIZE), f32)
    tile_kind = kept_in(tile_shape, f32)
    slots_kind = kept_in(slots_shape, f32)
    wide, slim = (heads, tokens, width), (heads, tokens, HEAD_SIZE)
    q, ko, vo, u = q[0, 0], ko[0, 0], vo[0, 0], u[0, 0]

    payload, ko_in, vo_in, q_first = call(
        pack_kernel,
        0,
        [(hbm, pinned(x)) for x in (kp[0], vp[0], ko, vo, q)],
        [kept_in((2 * part, kv_width), bf16)]
        + [kept_in(slim, bf16)] * 2
        + [kept_in((tokens, width), bf16)],
        [sems],
    )
    order = [0] + sorted(range(1, n), key=lambda k: -bin(k).count("1"))
    pays = [payload] + [swap(payload, n, k) for k in order[1:]]

    def across(x, k):
        return lax.ppermute(x, "prompt", [(i, i ^ k) for i in range(n_prompt)])

    small = [kept, pinned(spaces), spans, payoffs, across(kept, 1)]
    q_in, u_in, own, own_lse, tile, alive, length, qt, ut, scores, reward = call(
        functools.partial(own_kernel, group, 1),
        2,
        [(hbm, x) for x in small]
        + [(hbm, pinned(x)) for x in (q, u)]
        + [(vmem, x) for x in (q_first, ko_in, vo_in)],
        [kept_in(wide, bf16)] * 2
        + [stat, stat, tile_kind, slots_kind, tile_kind] + [kept_in((heads, HEAD_SIZE, rows), bf16)] * 2
        + [kept_in((heads, rows, tokens), f32), kept_in((EXTRA, HEAD_SIZE), f32)],
        [pltpu.SMEM(x.shape, x.dtype) for x in small]
        + [sems, pltpu.SemaphoreType.DMA((len(small),))],
    )
    k = 2
    while 4 * k < n_prompt:
        tile = tile + across(tile, k)
        k *= 2
    arriving = across(tile, k)
    att, ds, line, delta, *terms = call(
        functools.partial(prefix_kernel, n),
        5,
        [(vmem, x) for x in [q_in, u_in, own, own_lse, length, qt, ut, reward] + pays],
        [kept_in(wide, bf16), kept_in((heads, rows, prefix), bf16), stat, stat]
        + [kept_in((2 * heads * part + EXTRA, HEAD_SIZE), f32 if i == 0 else bf16) for i in range(n)],
        [],
    )
    def rest(begin, end, out, scratch):
        done = end - begin
        return call(
            functools.partial(rest_kernel, n, group, begin, end),
            6,
            [(vmem, x) for x in [u_in, ko_in, vo_in, att, ds, line, delta, qt, ut, scores] + pays],
            [kept_in((done, rows, HEAD_SIZE), f32)]
            + [kept_in((done, tokens, HEAD_SIZE), f32)] * 2
            + out,
            scratch,
        )

    received = [swap(t, n, k) for k, t in zip(order[1:], terms[1:])]
    (tile_sum,) = call(
        add_kernel, 0, [(vmem, tile), (vmem, arriving), (hbm, line)], [tile_kind], []
    )
    other = across(tile_sum, 2 * k)
    dq_sum, dko_sum, dvo_sum, attn_out = rest(0, heads, [given(q.shape)], [sems])
    total, weight = call(
        functools.partial(total_kernel, order),
        0,
        [(vmem, x) for x in [alive, terms[0]] + received],
        [kept_in((2 * heads * part, HEAD_SIZE), f32), tile_kind],
        [],
    )
    dq, dko, dvo, key_total, value_total = call(
        functools.partial(last_kernel, group),
        0,
        [(vmem, x) for x in [dq_sum, dko_sum, dvo_sum, tile_sum, total, weight, other]],
        [given(q.shape)] + [given(ko.shape)] * 2 + [given((part, kv_width))] * 2,
        [pltpu.VMEM(wide, bf16), pltpu.VMEM(slim, bf16), pltpu.VMEM(slim, bf16)]
        + [pltpu.VMEM((part, kv_width), bf16)] * 2
        + [sems],
    )
    return (
        attn_out[None, None],
        dq[None, None],
        dko[None, None],
        dvo[None, None],
        key_total[None],
        value_total[None],
    )


def solution(mesh):
    wide = P("prompt", "resp", None, None)
    rows = P("prompt", "resp", None)
    pair = P("prompt", "resp")
    return jax.shard_map(
        local,
        mesh=mesh,
        in_specs=(wide, wide, wide, wide, rows, rows, P("prompt"), P("prompt", None), pair, pair),
        out_specs=(wide, wide, wide, wide, rows, rows),
        check_vma=False,
    )
```

```python
import functools
import jax
import jax.numpy as jnp
from jax import lax
from jax.experimental import pallas as pl
from jax.experimental.pallas import tpu as pltpu
from jax.sharding import PartitionSpec as P

HEAD_SIZE = 128
BLOCK = 128
EXTRA = 16
SCALING = HEAD_SIZE**-0.5
POWER = SCALING * 1.4426950408889634
VMEM_LIMIT = 32 << 20
f32 = jnp.float32
bf16 = jnp.bfloat16
i32 = jnp.int32


def dot(a, b, ca, cb):
    return lax.dot_general(a, b, (((ca,), (cb,)), ((), ())), preferred_element_type=f32)


def swap(x, n, k):
    return lax.ppermute(x, "resp", [(i, i ^ k) for i in range(n)])


def columns_of(g, width):
    return pl.ds(pl.multiple_of(g * width, width), width)


def stacked(block):
    tokens, width = block.shape
    return jnp.concatenate(
        [
            block[t : t + BLOCK, i : i + HEAD_SIZE]
            for t in range(0, tokens, BLOCK)
            for i in range(0, width, HEAD_SIZE)
        ],
        0,
    )


def unstacked(x, group):
    x = x.astype(bf16)
    lines = [
        jnp.concatenate([x[t + i * BLOCK : t + (i + 1) * BLOCK] for i in range(group)], 1)
        for t in range(0, x.shape[0], group * BLOCK)
    ]
    return jnp.concatenate(lines, 0)


def row_blocks(rows, group):
    return [(slice(t, t + group * BLOCK), t // group + BLOCK) for t in range(0, rows, group * BLOCK)]


def spread(x, width):
    return jnp.concatenate([x] * (width // HEAD_SIZE), 1)


def with_ones(values):
    return jnp.concatenate([values, jnp.ones(values.shape, bf16)], 1)


def causal_mask(tokens, group):
    row = lax.broadcasted_iota(i32, (BLOCK, tokens), 0)
    key = lax.broadcasted_iota(i32, (BLOCK, tokens), 1)
    return jnp.concatenate(
        [key <= row + t for t in range(0, tokens, BLOCK) for _ in range(group)], 0
    )


def row_of(tile, index):
    row = lax.broadcasted_iota(i32, tile.shape, 0)
    return jnp.sum(jnp.where(row == index, tile, 0.0), 0, keepdims=True)


def pack_kernel(kp_hbm, vp_hbm, ko_hbm, vo_hbm, q_hbm, payload_ref, ko_ref, vo_ref, q_ref, sems):
    part = kp_hbm.shape[0]
    heads, width = ko_ref.shape[0], q_ref.shape[1]
    copies = [
        pltpu.make_async_copy(kp_hbm, payload_ref.at[:part], sems.at[0, 0]),
        pltpu.make_async_copy(vp_hbm, payload_ref.at[part:], sems.at[1, 0]),
        pltpu.make_async_copy(q_hbm.at[:, :width], q_ref, sems.at[2, 0]),
    ]
    for g in range(heads):
        cols = columns_of(g, HEAD_SIZE)
        copies.append(pltpu.make_async_copy(ko_hbm.at[:, cols], ko_ref.at[g], sems.at[3, g]))
        copies.append(pltpu.make_async_copy(vo_hbm.at[:, cols], vo_ref.at[g], sems.at[4, g]))
    for copy in copies:
        copy.start()
    for copy in copies:
        copy.wait()


def reward_rows(payoff):
    whole = jnp.full((EXTRA, HEAD_SIZE), payoff, f32)
    high = whole.astype(bf16).astype(f32)
    middle = (whole - high).astype(bf16).astype(f32)
    low = whole - high - middle
    row = lax.broadcasted_iota(i32, whole.shape, 0)
    return jnp.where(row == 0, high, jnp.where(row == 1, middle, jnp.where(row == 2, low, 0.0)))


def own_kernel(group, counts, *refs):
    small_hbm, refs = refs[: 4 + counts], refs[4 + counts :]
    q_hbm, u_hbm, q_first, ko_ref, vo_ref = refs[:5]
    q_ref, u_ref, att_ref, lse_ref, tile_ref, alive_ref, length_ref = refs[5:12]
    qt_ref, ut_ref, s_ref, reward_ref = refs[12:16]
    small_refs, sems, small_sems = refs[16:-2], refs[-2], refs[-1]
    heads, tokens, width = q_ref.shape

    def load(g):
        return pltpu.make_async_copy(q_hbm.at[:, columns_of(g, width)], q_ref.at[g], sems.at[0, g])

    def late_load(g):
        return pltpu.make_async_copy(u_hbm.at[:, columns_of(g, width)], u_ref.at[g], sems.at[1, g])

    small = [
        pltpu.make_async_copy(a, b, small_sems.at[i])
        for i, (a, b) in enumerate(zip(small_hbm, small_refs))
    ]
    for copy in small:
        copy.start()
    for g in range(1, heads):
        load(g).start()
    for g in range(heads):
        late_load(g).start()

    mask = causal_mask(tokens, group)

    def step(g, carry):
        q, ko, vo = stacked(q_ref[g]), ko_ref[g], vo_ref[g]
        s = jnp.where(mask, dot(q, ko, 1, 1) * POWER, -1e30)
        s_ref[g] = s
        top = jnp.max(s, 1, keepdims=True)
        e = jnp.exp2(s - top)
        both = dot(e.astype(bf16), with_ones(vo), 1, 0)
        mass = both[:, HEAD_SIZE:]
        att_ref[g] = both[:, :HEAD_SIZE] / mass
        lse_ref[g] = jnp.log2(mass) + top
        qt_ref[g] = q.T
        return carry

    q_ref[0] = q_first[...]
    step(0, 0)
    for copy in small:
        copy.wait()
    kept_ref, spaces_ref, spans_ref, payoff_ref = small_refs[:4]
    reward_ref[...] = reward_rows(payoff_ref[0, 0])
    member = lax.axis_index("resp")
    kept = kept_ref[0]
    row = lax.broadcasted_iota(i32, alive_ref.shape, 0)
    alive = jnp.zeros(alive_ref.shape, f32)
    own_alive = 0
    for i in range(spaces_ref.shape[1]):
        alive += jnp.where((row == spaces_ref[0, i]) & (i < kept), 1.0, 0.0)
        own_alive += jnp.where((spaces_ref[0, i] == member) & (i < kept), 1, 0)
    alive_ref[...] = alive
    count = kept + sum(r[0] for r in small_refs[4:])
    tile_ref[...] = jnp.full(tile_ref.shape, count.astype(f32))
    length = own_alive * spans_ref[0, 0] * BLOCK
    length_ref[...] = jnp.full(length_ref.shape, length.astype(f32))

    for g in range(1, heads):
        load(g).wait()
    lax.fori_loop(1, heads, step, 0, unroll=True)
    for g in range(heads):
        late_load(g).wait()
    for g in range(heads):
        ut_ref[g] = stacked(u_ref[g]).T


def prefix_kernel(n, *refs):
    q_ref, u_ref, own_ref, lse_ref, length_ref, qt_ref, ut_ref, reward_ref = refs[:8]
    pay_refs = refs[8 : 8 + n]
    out_ref, ds_ref, line_ref, delta_ref = refs[8 + n : 12 + n]
    term_refs = refs[12 + n :]
    for ref in term_refs:
        ref[-EXTRA:] = reward_ref[...].astype(ref.dtype)
    heads, tokens, width = q_ref.shape
    group = width // HEAD_SIZE
    part = pay_refs[0].shape[0] // 2
    token = lax.broadcasted_iota(i32, (tokens, HEAD_SIZE), 0).astype(f32)
    fits = token < length_ref[0:1]
    valid = jnp.concatenate(
        [fits[t : t + BLOCK] for t in range(0, tokens, BLOCK) for _ in range(group)], 0
    )

    def step(g, carry):
        cols = columns_of(g, HEAD_SIZE)
        keys = jnp.concatenate([r[:part, cols] for r in pay_refs], 0)
        values = jnp.concatenate([r[part : 2 * part, cols] for r in pay_refs], 0)
        q = stacked(q_ref[g])
        s = dot(q, keys, 1, 1)
        u = stacked(u_ref[g])
        dp = dot(u, values, 1, 1)
        own_lse = lse_ref[g]
        top = jnp.maximum(jnp.max(s, 1, keepdims=True) * POWER, own_lse)
        e = jnp.exp2(s * POWER - spread(top, s.shape[1]))
        both = dot(e.astype(bf16), with_ones(values), 1, 0)
        own_mass = jnp.exp2(own_lse - top)
        mass = both[:, HEAD_SIZE:] + own_mass
        inverse = jnp.where(valid, 1.0 / mass, 0.0)
        attended = (both[:, :HEAD_SIZE] + own_ref[g] * own_mass) * inverse
        out_ref[g] = unstacked(attended, group)
        p = e * spread(inverse, s.shape[1])
        delta = jnp.sum(u.astype(f32) * attended, 1, keepdims=True)
        ds = (p * (dp - delta)).astype(bf16)
        ds_ref[g] = ds
        line_ref[g] = jnp.where(valid, top + jnp.log2(mass), 1e30)
        delta_ref[g] = jnp.broadcast_to(delta, top.shape)
        dk = dot(qt_ref[g], ds, 1, 0).T * SCALING
        dv = dot(ut_ref[g], p.astype(bf16), 1, 0).T
        for k, ref in enumerate(term_refs):
            at = 2 * g * part
            ref[pl.ds(at, part)] = dk[k * part : (k + 1) * part].astype(ref.dtype)
            ref[pl.ds(at + part, part)] = dv[k * part : (k + 1) * part].astype(ref.dtype)
        return carry

    lax.fori_loop(0, heads, step, 0, unroll=True)


def add_kernel(tile_ref, recv_ref, after_ref, sum_ref):
    sum_ref[...] = tile_ref[...] + recv_ref[...]


def rest_kernel(n, group, begin, end, *refs):
    u_ref, ko_ref, vo_ref, att_ref, ds_ref, line_ref, delta_ref = refs[:7]
    qt_ref, ut_ref, s_ref = refs[7:10]
    pay_refs = refs[10 : 10 + n]
    dq_ref, dko_ref, dvo_ref = refs[10 + n : 13 + n]
    out_hbm, sems = refs[13 + n :] if len(refs) > 13 + n else (None, None)
    _, tokens, width = u_ref.shape
    part = pay_refs[0].shape[0] // 2

    def store(g):
        return pltpu.make_async_copy(att_ref.at[g], out_hbm.at[:, columns_of(g, width)], sems.at[0, g])

    stored = range(u_ref.shape[0]) if out_hbm is not None else ()
    for g in stored:
        store(g).start()

    def step(g, carry):
        cols = columns_of(g, HEAD_SIZE)
        keys = jnp.concatenate([r[:part, cols] for r in pay_refs], 0)
        u, ko, vo = stacked(u_ref[g]), ko_ref[g], vo_ref[g]
        p = jnp.exp2(s_ref[g] - spread(line_ref[g], tokens))
        dp = dot(u, vo, 1, 1)
        ds = (p * (dp - spread(delta_ref[g], tokens))).astype(bf16)
        all_ds = jnp.concatenate([ds_ref[g], ds], 1)
        dq_ref[g - begin] = dot(all_ds, jnp.concatenate([keys, ko], 0), 1, 0)
        dk = dot(qt_ref[g], ds, 1, 0)
        dv = dot(ut_ref[g], p.astype(bf16), 1, 0)
        dko_ref[g - begin] = dk.T
        dvo_ref[g - begin] = dv.T
        return carry

    lax.fori_loop(begin, end, step, 0, unroll=True)
    for g in stored:
        store(g).wait()


def total_kernel(order, alive_ref, *refs):
    term_refs, (total_ref, weight_ref) = refs[:-2], refs[-2:]
    alive = alive_ref[...]
    member = lax.axis_index("resp")
    rewards = [jnp.sum(r[-EXTRA:].astype(f32), 0, keepdims=True) for r in term_refs]
    total = sum(reward * row_of(alive, member ^ k) for k, reward in zip(order, rewards))
    mean = total / jnp.sum(alive, 0, keepdims=True)
    weights = [reward - mean for reward in rewards]
    rows = total_ref.shape[0]
    total_ref[...] = sum(r[:rows].astype(f32) * w for r, w in zip(term_refs, weights))
    weight_ref[...] = jnp.broadcast_to(weights[0], weight_ref.shape)


def last_kernel(group, *refs):
    dq_ref, dko_ref, dvo_ref, sum_ref, total_ref, weight_ref, recv_ref = refs[:7]
    dq_hbm, dko_hbm, dvo_hbm, key_hbm, value_hbm = refs[7:12]
    dq_low, dko_low, dvo_low, key_ref, value_ref, sems = refs[12:]
    heads = dko_ref.shape[0]
    part = key_ref.shape[0]
    width = group * HEAD_SIZE

    def store(g):
        return pltpu.make_async_copy(dq_low.at[g], dq_hbm.at[:, columns_of(g, width)], sems.at[0, g])

    whole = [
        pltpu.make_async_copy(a, b, sems.at[1, i])
        for i, (a, b) in enumerate(
            ((dko_low, dko_hbm), (dvo_low, dvo_hbm), (key_ref, key_hbm), (value_ref, value_hbm))
        )
    ]
    share = 1.0 / (sum_ref[0:1] + recv_ref[0:1])
    weight = weight_ref[0:1] * share
    for g in range(heads):
        dq_low[g] = unstacked(dq_ref[g] * (weight * SCALING), group)
        store(g).start()
    for g in range(heads):
        cols = slice(g * HEAD_SIZE, (g + 1) * HEAD_SIZE)
        dko_low[:, cols] = (dko_ref[g] * (weight * SCALING)).astype(bf16)
        dvo_low[:, cols] = (dvo_ref[g] * weight).astype(bf16)
        for at, ref in ((2 * g * part, key_ref), ((2 * g + 1) * part, value_ref)):
            ref[:, cols] = (total_ref[at : at + part] * share).astype(bf16)
    for copy in whole:
        copy.start()
    for g in range(heads):
        store(g).wait()
    for copy in whole:
        copy.wait()


def local(q, ko, vo, u, kp, vp, kept, spaces, spans, payoffs):
    n = lax.axis_size("resp")
    n_prompt = lax.axis_size("prompt")
    tokens = q.shape[2]
    kv_width = ko.shape[3]
    heads = kv_width // HEAD_SIZE
    group = q.shape[3] // kv_width
    width = group * HEAD_SIZE
    rows = group * tokens
    part = kp.shape[1]
    prefix = n * part
    tile_shape = (8, HEAD_SIZE)
    slots_shape = (-(-n // 8) * 8, HEAD_SIZE)

    vmem = pl.BlockSpec(memory_space=pltpu.VMEM)
    hbm = pl.BlockSpec(memory_space=pl.ANY)

    def pinned(x):
        return pltpu.with_memory_space_constraint(x, pltpu.HBM)

    def call(kernel, units, ins, out, scratch):
        return pl.pallas_call(
            kernel,
            in_specs=[spec for spec, _ in ins],
            out_specs=[spec for spec, _ in out],
            out_shape=[shape for _, shape in out],
            scratch_shapes=scratch,
            compiler_params=pltpu.CompilerParams(vmem_limit_bytes=VMEM_LIMIT),
            cost_estimate=pl.CostEstimate(
                flops=units * 2 * heads * rows * tokens * HEAD_SIZE,
                bytes_accessed=1 << 20,
                transcendentals=0,
            ),
        )(*[x for _, x in ins])

    def kept_in(shape, kind):
        return (vmem, pltpu.VMEM(shape, kind))

    def given(shape, kind=bf16, spec=hbm):
        return (spec, jax.ShapeDtypeStruct(shape, kind))

    sems = pltpu.SemaphoreType.DMA((5, heads))
    stat = kept_in((heads, rows, HEAD_SIZE), f32)
    tile_kind = kept_in(tile_shape, f32)
    slots_kind = kept_in(slots_shape, f32)
    wide, slim = (heads, tokens, width), (heads, tokens, HEAD_SIZE)
    q, ko, vo, u = q[0, 0], ko[0, 0], vo[0, 0], u[0, 0]

    payload, ko_in, vo_in, q_first = call(
        pack_kernel,
        0,
        [(hbm, pinned(x)) for x in (kp[0], vp[0], ko, vo, q)],
        [kept_in((2 * part, kv_width), bf16)]
        + [kept_in(slim, bf16)] * 2
        + [kept_in((tokens, width), bf16)],
        [sems],
    )
    order = [0] + sorted(range(1, n), key=lambda k: -bin(k).count("1"))
    pays = [payload] + [swap(payload, n, k) for k in order[1:]]

    def across(x, k):
        return lax.ppermute(x, "prompt", [(i, i ^ k) for i in range(n_prompt)])

    small = [kept, pinned(spaces), spans, payoffs, across(kept, 1)]
    q_in, u_in, own, own_lse, tile, alive, length, qt, ut, scores, reward = call(
        functools.partial(own_kernel, group, 1),
        2,
        [(hbm, x) for x in small]
        + [(hbm, pinned(x)) for x in (q, u)]
        + [(vmem, x) for x in (q_first, ko_in, vo_in)],
        [kept_in(wide, bf16)] * 2
        + [stat, stat, tile_kind, slots_kind, tile_kind] + [kept_in((heads, HEAD_SIZE, rows), bf16)] * 2
        + [kept_in((heads, rows, tokens), f32), kept_in((EXTRA, HEAD_SIZE), f32)],
        [pltpu.SMEM(x.shape, x.dtype) for x in small]
        + [sems, pltpu.SemaphoreType.DMA((len(small),))],
    )
    k = 2
    while 4 * k < n_prompt:
        tile = tile + across(tile, k)
        k *= 2
    arriving = across(tile, k)
    att, ds, line, delta, *terms = call(
        functools.partial(prefix_kernel, n),
        5,
        [(vmem, x) for x in [q_in, u_in, own, own_lse, length, qt, ut, reward] + pays],
        [kept_in(wide, bf16), kept_in((heads, rows, prefix), bf16), stat, stat]
        + [kept_in((2 * heads * part + EXTRA, HEAD_SIZE), f32 if i == 0 else bf16) for i in range(n)],
        [],
    )
    def rest(begin, end, out, scratch):
        done = end - begin
        return call(
            functools.partial(rest_kernel, n, group, begin, end),
            6,
            [(vmem, x) for x in [u_in, ko_in, vo_in, att, ds, line, delta, qt, ut, scores] + pays],
            [kept_in((done, rows, HEAD_SIZE), f32)]
            + [kept_in((done, tokens, HEAD_SIZE), f32)] * 2
            + out,
            scratch,
        )

    received = [swap(t, n, k) for k, t in zip(order[1:], terms[1:])]
    (tile_sum,) = call(
        add_kernel, 0, [(vmem, tile), (vmem, arriving), (hbm, line)], [tile_kind], []
    )
    other = across(tile_sum, 2 * k)
    dq_sum, dko_sum, dvo_sum, attn_out = rest(0, heads, [given(q.shape)], [sems])
    total, weight = call(
        functools.partial(total_kernel, order),
        0,
        [(vmem, x) for x in [alive, terms[0]] + received],
        [kept_in((2 * heads * part, HEAD_SIZE), f32), tile_kind],
        [],
    )
    dq, dko, dvo, key_total, value_total = call(
        functools.partial(last_kernel, group),
        0,
        [(vmem, x) for x in [dq_sum, dko_sum, dvo_sum, tile_sum, total, weight, other]],
        [given(q.shape)] + [given(ko.shape)] * 2 + [given((part, kv_width))] * 2,
        [pltpu.VMEM(wide, bf16)]
        + [pltpu.VMEM((tokens, kv_width), bf16)] * 2
        + [pltpu.VMEM((part, kv_width), bf16)] * 2
        + [sems],
    )
    return (
        attn_out[None, None],
        dq[None, None],
        dko[None, None],
        dvo[None, None],
        key_total[None],
        value_total[None],
    )


def solution(mesh):
    wide = P("prompt", "resp", None, None)
    rows = P("prompt", "resp", None)
    pair = P("prompt", "resp")
    return jax.shard_map(
        local,
        mesh=mesh,
        in_specs=(wide, wide, wide, wide, rows, rows, P("prompt"), P("prompt", None), pair, pair),
        out_specs=(wide, wide, wide, wide, rows, rows),
        check_vma=False,
    )
```

```python
import functools
import jax
import jax.numpy as jnp
from jax import lax
from jax.experimental import pallas as pl
from jax.experimental.pallas import tpu as pltpu
from jax.sharding import PartitionSpec as P

HEAD_SIZE = 128
BLOCK = 128
EXTRA = 16
SCALING = HEAD_SIZE**-0.5
POWER = SCALING * 1.4426950408889634
VMEM_LIMIT = 32 << 20
f32 = jnp.float32
bf16 = jnp.bfloat16
i32 = jnp.int32


def dot(a, b, ca, cb):
    return lax.dot_general(a, b, (((ca,), (cb,)), ((), ())), preferred_element_type=f32)


def swap(x, n, k):
    return lax.ppermute(x, "resp", [(i, i ^ k) for i in range(n)])


def columns_of(g, width):
    return pl.ds(pl.multiple_of(g * width, width), width)


def stacked(block):
    tokens, width = block.shape
    return jnp.concatenate(
        [
            block[t : t + BLOCK, i : i + HEAD_SIZE]
            for t in range(0, tokens, BLOCK)
            for i in range(0, width, HEAD_SIZE)
        ],
        0,
    )


def unstacked(x, group):
    x = x.astype(bf16)
    lines = [
        jnp.concatenate([x[t + i * BLOCK : t + (i + 1) * BLOCK] for i in range(group)], 1)
        for t in range(0, x.shape[0], group * BLOCK)
    ]
    return jnp.concatenate(lines, 0)


def row_blocks(rows, group):
    return [(slice(t, t + group * BLOCK), t // group + BLOCK) for t in range(0, rows, group * BLOCK)]


def spread(x, width):
    return jnp.concatenate([x] * (width // HEAD_SIZE), 1)


def with_ones(values):
    return jnp.concatenate([values, jnp.ones(values.shape, bf16)], 1)


def causal_mask(tokens, group):
    row = lax.broadcasted_iota(i32, (BLOCK, tokens), 0)
    key = lax.broadcasted_iota(i32, (BLOCK, tokens), 1)
    return jnp.concatenate(
        [key <= row + t for t in range(0, tokens, BLOCK) for _ in range(group)], 0
    )


def row_of(tile, index):
    row = lax.broadcasted_iota(i32, tile.shape, 0)
    return jnp.sum(jnp.where(row == index, tile, 0.0), 0, keepdims=True)


def pack_kernel(kp_hbm, vp_hbm, ko_hbm, vo_hbm, q_hbm, u_hbm, payload_ref, ko_ref, vo_ref, q_ref, u_ref, sems):
    part = kp_hbm.shape[0]
    width = q_ref.shape[2]
    copies = [
        pltpu.make_async_copy(kp_hbm, payload_ref.at[:part], sems.at[0, 0]),
        pltpu.make_async_copy(vp_hbm, payload_ref.at[part:], sems.at[0, 1]),
    ]
    for g in range(q_ref.shape[0]):
        cols = columns_of(g, width)
        copies.append(pltpu.make_async_copy(q_hbm.at[:, cols], q_ref.at[g], sems.at[2, g]))
        copies.append(pltpu.make_async_copy(u_hbm.at[:, cols], u_ref.at[g], sems.at[1, g]))
    copies.append(pltpu.make_async_copy(ko_hbm, ko_ref, sems.at[3, 0]))
    copies.append(pltpu.make_async_copy(vo_hbm, vo_ref, sems.at[4, 0]))
    for copy in copies:
        copy.start()
    for copy in copies:
        copy.wait()


def reward_rows(payoff):
    whole = jnp.full((EXTRA, HEAD_SIZE), payoff, f32)
    high = whole.astype(bf16).astype(f32)
    middle = (whole - high).astype(bf16).astype(f32)
    low = whole - high - middle
    row = lax.broadcasted_iota(i32, whole.shape, 0)
    return jnp.where(row == 0, high, jnp.where(row == 1, middle, jnp.where(row == 2, low, 0.0)))


def own_kernel(group, counts, *refs):
    kept_ref, spans_ref, payoff_ref = refs[:3]
    small_hbm, refs = refs[3 : 4 + counts], refs[4 + counts :]
    u_ref, q_ref, ko_ref, vo_ref = refs[:4]
    att_ref, lse_ref, tile_ref, alive_ref, length_ref = refs[4:9]
    qt_ref, ut_ref, s_ref, reward_ref = refs[9:13]
    small_refs, small_sems = refs[13:-1], refs[-1]
    heads, tokens, width = q_ref.shape

    small = [
        pltpu.make_async_copy(a, b, small_sems.at[i])
        for i, (a, b) in enumerate(zip(small_hbm, small_refs))
    ]
    for copy in small:
        copy.start()

    mask = causal_mask(tokens, group)

    def step(g, carry):
        cols = columns_of(g, HEAD_SIZE)
        q, ko, vo = stacked(q_ref[g]), ko_ref[:, cols], vo_ref[:, cols]
        s = jnp.where(mask, dot(q, ko, 1, 1) * POWER, -1e30)
        s_ref[g] = s
        top = jnp.max(s, 1, keepdims=True)
        e = jnp.exp2(s - top)
        both = dot(e.astype(bf16), with_ones(vo), 1, 0)
        mass = both[:, HEAD_SIZE:]
        att_ref[g] = both[:, :HEAD_SIZE] / mass
        lse_ref[g] = jnp.log2(mass) + top
        qt_ref[g] = q.T
        ut_ref[g] = stacked(u_ref[g]).T
        return carry

    lax.fori_loop(0, heads, step, 0, unroll=True)
    for copy in small:
        copy.wait()
    spaces_ref = small_refs[0]
    reward_ref[...] = reward_rows(payoff_ref[0, 0])
    member = lax.axis_index("resp")
    kept = kept_ref[0]
    row = lax.broadcasted_iota(i32, alive_ref.shape, 0)
    alive = jnp.zeros(alive_ref.shape, f32)
    own_alive = 0
    for i in range(spaces_ref.shape[1]):
        alive += jnp.where((row == spaces_ref[0, i]) & (i < kept), 1.0, 0.0)
        own_alive += jnp.where((spaces_ref[0, i] == member) & (i < kept), 1, 0)
    alive_ref[...] = alive
    count = kept + sum(r[0] for r in small_refs[1:])
    tile_ref[...] = jnp.full(tile_ref.shape, count.astype(f32))
    length = own_alive * spans_ref[0, 0] * BLOCK
    length_ref[...] = jnp.full(length_ref.shape, length.astype(f32))


def prefix_kernel(n, *refs):
    q_ref, u_ref, own_ref, lse_ref, length_ref, qt_ref, ut_ref, reward_ref = refs[:8]
    pay_refs = refs[8 : 8 + n]
    out_ref, ds_ref, line_ref, delta_ref = refs[8 + n : 12 + n]
    term_refs = refs[12 + n :]
    for ref in term_refs:
        ref[-EXTRA:] = reward_ref[...].astype(ref.dtype)
    heads, tokens, width = q_ref.shape
    group = width // HEAD_SIZE
    part = pay_refs[0].shape[0] // 2
    token = lax.broadcasted_iota(i32, (tokens, HEAD_SIZE), 0).astype(f32)
    fits = token < length_ref[0:1]
    valid = jnp.concatenate(
        [fits[t : t + BLOCK] for t in range(0, tokens, BLOCK) for _ in range(group)], 0
    )

    def step(g, carry):
        cols = columns_of(g, HEAD_SIZE)
        keys = jnp.concatenate([r[:part, cols] for r in pay_refs], 0)
        values = jnp.concatenate([r[part : 2 * part, cols] for r in pay_refs], 0)
        q = stacked(q_ref[g])
        s = dot(q, keys, 1, 1)
        u = stacked(u_ref[g])
        dp = dot(u, values, 1, 1)
        own_lse = lse_ref[g]
        top = jnp.maximum(jnp.max(s, 1, keepdims=True) * POWER, own_lse)
        e = jnp.exp2(s * POWER - spread(top, s.shape[1]))
        both = dot(e.astype(bf16), with_ones(values), 1, 0)
        own_mass = jnp.exp2(own_lse - top)
        mass = both[:, HEAD_SIZE:] + own_mass
        inverse = jnp.where(valid, 1.0 / mass, 0.0)
        attended = (both[:, :HEAD_SIZE] + own_ref[g] * own_mass) * inverse
        out_ref[g] = unstacked(attended, group)
        p = e * spread(inverse, s.shape[1])
        delta = jnp.sum(u.astype(f32) * attended, 1, keepdims=True)
        ds = (p * (dp - delta)).astype(bf16)
        ds_ref[g] = ds
        line_ref[g] = jnp.where(valid, top + jnp.log2(mass), 1e30)
        delta_ref[g] = jnp.broadcast_to(delta, top.shape)
        dk = dot(qt_ref[g], ds, 1, 0).T * SCALING
        dv = dot(ut_ref[g], p.astype(bf16), 1, 0).T
        for k, ref in enumerate(term_refs):
            at = 2 * g * part
            ref[pl.ds(at, part)] = dk[k * part : (k + 1) * part].astype(ref.dtype)
            ref[pl.ds(at + part, part)] = dv[k * part : (k + 1) * part].astype(ref.dtype)
        return carry

    lax.fori_loop(0, heads, step, 0, unroll=True)


def add_kernel(tile_ref, recv_ref, after_ref, sum_ref):
    sum_ref[...] = tile_ref[...] + recv_ref[...]


def rest_kernel(n, group, begin, end, *refs):
    u_ref, ko_ref, vo_ref, att_ref, ds_ref, line_ref, delta_ref = refs[:7]
    qt_ref, ut_ref, s_ref = refs[7:10]
    pay_refs = refs[10 : 10 + n]
    dq_ref, dko_ref, dvo_ref = refs[10 + n : 13 + n]
    out_hbm, sems = refs[13 + n :] if len(refs) > 13 + n else (None, None)
    _, tokens, width = u_ref.shape
    part = pay_refs[0].shape[0] // 2

    def store(g):
        return pltpu.make_async_copy(att_ref.at[g], out_hbm.at[:, columns_of(g, width)], sems.at[0, g])

    stored = range(u_ref.shape[0]) if out_hbm is not None else ()
    for g in stored:
        store(g).start()

    def step(g, carry):
        cols = columns_of(g, HEAD_SIZE)
        keys = jnp.concatenate([r[:part, cols] for r in pay_refs], 0)
        u, ko, vo = stacked(u_ref[g]), ko_ref[:, cols], vo_ref[:, cols]
        p = jnp.exp2(s_ref[g] - spread(line_ref[g], tokens))
        dp = dot(u, vo, 1, 1)
        ds = (p * (dp - spread(delta_ref[g], tokens))).astype(bf16)
        all_ds = jnp.concatenate([ds_ref[g], ds], 1)
        dq_ref[g - begin] = dot(all_ds, jnp.concatenate([keys, ko], 0), 1, 0)
        dk = dot(qt_ref[g], ds, 1, 0)
        dv = dot(ut_ref[g], p.astype(bf16), 1, 0)
        dko_ref[g - begin] = dk.T
        dvo_ref[g - begin] = dv.T
        return carry

    lax.fori_loop(begin, end, step, 0, unroll=True)
    for g in stored:
        store(g).wait()


def total_kernel(order, alive_ref, *refs):
    term_refs, (total_ref, weight_ref) = refs[:-2], refs[-2:]
    alive = alive_ref[...]
    member = lax.axis_index("resp")
    rewards = [jnp.sum(r[-EXTRA:].astype(f32), 0, keepdims=True) for r in term_refs]
    total = sum(reward * row_of(alive, member ^ k) for k, reward in zip(order, rewards))
    mean = total / jnp.sum(alive, 0, keepdims=True)
    weights = [reward - mean for reward in rewards]
    rows = total_ref.shape[0]
    total_ref[...] = sum(r[:rows].astype(f32) * w for r, w in zip(term_refs, weights))
    weight_ref[...] = jnp.broadcast_to(weights[0], weight_ref.shape)


def last_kernel(group, *refs):
    dq_ref, dko_ref, dvo_ref, sum_ref, total_ref, weight_ref, recv_ref = refs[:7]
    dq_hbm, dko_hbm, dvo_hbm, key_hbm, value_hbm = refs[7:12]
    dq_low, dko_low, dvo_low, key_ref, value_ref, sems = refs[12:]
    heads = dko_ref.shape[0]
    part = key_ref.shape[0]
    width = group * HEAD_SIZE

    def store(g):
        return pltpu.make_async_copy(dq_low.at[g], dq_hbm.at[:, columns_of(g, width)], sems.at[0, g])

    whole = [
        pltpu.make_async_copy(a, b, sems.at[1, i])
        for i, (a, b) in enumerate(
            ((dko_low, dko_hbm), (dvo_low, dvo_hbm), (key_ref, key_hbm), (value_ref, value_hbm))
        )
    ]
    share = 1.0 / (sum_ref[0:1] + recv_ref[0:1])
    weight = weight_ref[0:1] * share
    for g in range(heads):
        dq_low[g] = unstacked(dq_ref[g] * (weight * SCALING), group)
        store(g).start()
    for g in range(heads):
        cols = slice(g * HEAD_SIZE, (g + 1) * HEAD_SIZE)
        dko_low[:, cols] = (dko_ref[g] * (weight * SCALING)).astype(bf16)
        dvo_low[:, cols] = (dvo_ref[g] * weight).astype(bf16)
        for at, ref in ((2 * g * part, key_ref), ((2 * g + 1) * part, value_ref)):
            ref[:, cols] = (total_ref[at : at + part] * share).astype(bf16)
    for copy in whole:
        copy.start()
    for g in range(heads):
        store(g).wait()
    for copy in whole:
        copy.wait()


def local(q, ko, vo, u, kp, vp, kept, spaces, spans, payoffs):
    n = lax.axis_size("resp")
    n_prompt = lax.axis_size("prompt")
    tokens = q.shape[2]
    kv_width = ko.shape[3]
    heads = kv_width // HEAD_SIZE
    group = q.shape[3] // kv_width
    width = group * HEAD_SIZE
    rows = group * tokens
    part = kp.shape[1]
    prefix = n * part
    tile_shape = (8, HEAD_SIZE)
    slots_shape = (-(-n // 8) * 8, HEAD_SIZE)

    vmem = pl.BlockSpec(memory_space=pltpu.VMEM)
    hbm = pl.BlockSpec(memory_space=pl.ANY)
    scalar = pl.BlockSpec(memory_space=pltpu.SMEM)

    def pinned(x):
        return pltpu.with_memory_space_constraint(x, pltpu.HBM)

    def call(kernel, units, ins, out, scratch):
        return pl.pallas_call(
            kernel,
            in_specs=[spec for spec, _ in ins],
            out_specs=[spec for spec, _ in out],
            out_shape=[shape for _, shape in out],
            scratch_shapes=scratch,
            compiler_params=pltpu.CompilerParams(vmem_limit_bytes=VMEM_LIMIT),
            cost_estimate=pl.CostEstimate(
                flops=units * 2 * heads * rows * tokens * HEAD_SIZE,
                bytes_accessed=1 << 20,
                transcendentals=0,
            ),
        )(*[x for _, x in ins])

    def kept_in(shape, kind):
        return (vmem, pltpu.VMEM(shape, kind))

    def given(shape, kind=bf16, spec=hbm):
        return (spec, jax.ShapeDtypeStruct(shape, kind))

    sems = pltpu.SemaphoreType.DMA((5, heads))
    stat = kept_in((heads, rows, HEAD_SIZE), f32)
    tile_kind = kept_in(tile_shape, f32)
    slots_kind = kept_in(slots_shape, f32)
    wide, slim = (heads, tokens, width), (heads, tokens, HEAD_SIZE)
    q, ko, vo, u = q[0, 0], ko[0, 0], vo[0, 0], u[0, 0]

    payload, ko_in, vo_in, q_in, u_in = call(
        pack_kernel,
        0,
        [(hbm, pinned(x)) for x in (kp[0], vp[0], ko, vo, q, u)],
        [kept_in((2 * part, kv_width), bf16)]
        + [kept_in((tokens, kv_width), bf16)] * 2
        + [kept_in(wide, bf16)] * 2,
        [sems],
    )
    order = [0] + sorted(range(1, n), key=lambda k: -bin(k).count("1"))
    pays = [payload] + [swap(payload, n, k) for k in order[1:]]

    def across(x, k):
        return lax.ppermute(x, "prompt", [(i, i ^ k) for i in range(n_prompt)])

    small = [pinned(spaces), across(kept, 1)]
    own, own_lse, tile, alive, length, qt, ut, scores, reward = call(
        functools.partial(own_kernel, group, 1),
        2,
        [(scalar, x) for x in (kept, spans, payoffs)]
        + [(hbm, x) for x in small]
        + [(vmem, x) for x in (u_in, q_in, ko_in, vo_in)],
        [stat, stat, tile_kind, slots_kind, tile_kind] + [kept_in((heads, HEAD_SIZE, rows), bf16)] * 2
        + [kept_in((heads, rows, tokens), f32), kept_in((EXTRA, HEAD_SIZE), f32)],
        [pltpu.SMEM(x.shape, x.dtype) for x in small]
        + [pltpu.SemaphoreType.DMA((len(small),))],
    )
    k = 2
    while 4 * k < n_prompt:
        tile = tile + across(tile, k)
        k *= 2
    arriving = across(tile, k)
    att, ds, line, delta, *terms = call(
        functools.partial(prefix_kernel, n),
        5,
        [(vmem, x) for x in [q_in, u_in, own, own_lse, length, qt, ut, reward] + pays],
        [kept_in(wide, bf16), kept_in((heads, rows, prefix), bf16), stat, stat]
        + [kept_in((2 * heads * part + EXTRA, HEAD_SIZE), f32 if i == 0 else bf16) for i in range(n)],
        [],
    )
    def rest(begin, end, out, scratch):
        done = end - begin
        return call(
            functools.partial(rest_kernel, n, group, begin, end),
            6,
            [(vmem, x) for x in [u_in, ko_in, vo_in, att, ds, line, delta, qt, ut, scores] + pays],
            [kept_in((done, rows, HEAD_SIZE), f32)]
            + [kept_in((done, tokens, HEAD_SIZE), f32)] * 2
            + out,
            scratch,
        )

    received = [swap(t, n, k) for k, t in zip(order[1:], terms[1:])]
    (tile_sum,) = call(
        add_kernel, 0, [(vmem, tile), (vmem, arriving), (hbm, line)], [tile_kind], []
    )
    other = across(tile_sum, 2 * k)
    dq_sum, dko_sum, dvo_sum, attn_out = rest(0, heads, [given(q.shape)], [sems])
    total, weight = call(
        functools.partial(total_kernel, order),
        0,
        [(vmem, x) for x in [alive, terms[0]] + received],
        [kept_in((2 * heads * part, HEAD_SIZE), f32), tile_kind],
        [],
    )
    dq, dko, dvo, key_total, value_total = call(
        functools.partial(last_kernel, group),
        0,
        [(vmem, x) for x in [dq_sum, dko_sum, dvo_sum, tile_sum, total, weight, other]],
        [given(q.shape)] + [given(ko.shape)] * 2 + [given((part, kv_width))] * 2,
        [pltpu.VMEM(wide, bf16)]
        + [pltpu.VMEM((tokens, kv_width), bf16)] * 2
        + [pltpu.VMEM((part, kv_width), bf16)] * 2
        + [sems],
    )
    return (
        attn_out[None, None],
        dq[None, None],
        dko[None, None],
        dvo[None, None],
        key_total[None],
        value_total[None],
    )


def solution(mesh):
    wide = P("prompt", "resp", None, None)
    rows = P("prompt", "resp", None)
    pair = P("prompt", "resp")
    return jax.shard_map(
        local,
        mesh=mesh,
        in_specs=(wide, wide, wide, wide, rows, rows, P("prompt"), P("prompt", None), pair, pair),
        out_specs=(wide, wide, wide, wide, rows, rows),
        check_vma=False,
    )
```

```python
import functools
import jax
import jax.numpy as jnp
from jax import lax
from jax.experimental import pallas as pl
from jax.experimental.pallas import tpu as pltpu
from jax.sharding import PartitionSpec as P

HEAD_SIZE = 128
BLOCK = 128
EXTRA = 16
SCALING = HEAD_SIZE**-0.5
POWER = SCALING * 1.4426950408889634
VMEM_LIMIT = 32 << 20
f32 = jnp.float32
bf16 = jnp.bfloat16
i32 = jnp.int32


def dot(a, b, ca, cb):
    return lax.dot_general(a, b, (((ca,), (cb,)), ((), ())), preferred_element_type=f32)


def swap(x, n, k):
    return lax.ppermute(x, "resp", [(i, i ^ k) for i in range(n)])


def columns_of(g, width):
    return pl.ds(pl.multiple_of(g * width, width), width)


def stacked(block):
    tokens, width = block.shape
    return jnp.concatenate(
        [
            block[t : t + BLOCK, i : i + HEAD_SIZE]
            for t in range(0, tokens, BLOCK)
            for i in range(0, width, HEAD_SIZE)
        ],
        0,
    )


def unstacked(x, group):
    x = x.astype(bf16)
    lines = [
        jnp.concatenate([x[t + i * BLOCK : t + (i + 1) * BLOCK] for i in range(group)], 1)
        for t in range(0, x.shape[0], group * BLOCK)
    ]
    return jnp.concatenate(lines, 0)


def row_blocks(rows, group):
    return [(slice(t, t + group * BLOCK), t // group + BLOCK) for t in range(0, rows, group * BLOCK)]


def spread(x, width):
    return jnp.concatenate([x] * (width // HEAD_SIZE), 1)


def with_ones(values):
    return jnp.concatenate([values, jnp.ones(values.shape, bf16)], 1)


def causal_mask(tokens, group):
    row = lax.broadcasted_iota(i32, (BLOCK, tokens), 0)
    key = lax.broadcasted_iota(i32, (BLOCK, tokens), 1)
    return jnp.concatenate(
        [key <= row + t for t in range(0, tokens, BLOCK) for _ in range(group)], 0
    )


def row_of(tile, index):
    row = lax.broadcasted_iota(i32, tile.shape, 0)
    return jnp.sum(jnp.where(row == index, tile, 0.0), 0, keepdims=True)


def pack_kernel(kp_hbm, vp_hbm, payload_ref, sems):
    part = kp_hbm.shape[0]
    copies = [
        pltpu.make_async_copy(kp_hbm, payload_ref.at[:part], sems.at[0, 0]),
        pltpu.make_async_copy(vp_hbm, payload_ref.at[part:], sems.at[0, 1]),
    ]
    for copy in copies:
        copy.start()
    for copy in copies:
        copy.wait()


def reward_rows(payoff):
    whole = jnp.full((EXTRA, HEAD_SIZE), payoff, f32)
    high = whole.astype(bf16).astype(f32)
    middle = (whole - high).astype(bf16).astype(f32)
    low = whole - high - middle
    row = lax.broadcasted_iota(i32, whole.shape, 0)
    return jnp.where(row == 0, high, jnp.where(row == 1, middle, jnp.where(row == 2, low, 0.0)))


def own_kernel(group, counts, *refs):
    kept_ref, spans_ref, payoff_ref = refs[:3]
    width = group * HEAD_SIZE
    small_hbm, refs = refs[3 : 4 + counts], refs[4 + counts :]
    u_ref, q_ref, ko_ref, vo_ref = refs[:4]
    att_ref, lse_ref, tile_ref, alive_ref, length_ref = refs[4:9]
    qt_ref, ut_ref, s_ref, reward_ref = refs[9:13]
    small_refs, small_sems = refs[13:-1], refs[-1]
    tokens = q_ref.shape[0]
    heads = q_ref.shape[1] // width

    small = [
        pltpu.make_async_copy(a, b, small_sems.at[i])
        for i, (a, b) in enumerate(zip(small_hbm, small_refs))
    ]
    for copy in small:
        copy.start()

    mask = causal_mask(tokens, group)

    def step(g, carry):
        cols = columns_of(g, HEAD_SIZE)
        q, ko, vo = stacked(q_ref[:, columns_of(g, width)]), ko_ref[:, cols], vo_ref[:, cols]
        s = jnp.where(mask, dot(q, ko, 1, 1) * POWER, -1e30)
        s_ref[g] = s
        top = jnp.max(s, 1, keepdims=True)
        e = jnp.exp2(s - top)
        both = dot(e.astype(bf16), with_ones(vo), 1, 0)
        mass = both[:, HEAD_SIZE:]
        att_ref[g] = both[:, :HEAD_SIZE] / mass
        lse_ref[g] = jnp.log2(mass) + top
        qt_ref[g] = q.T
        ut_ref[g] = stacked(u_ref[:, columns_of(g, width)]).T
        return carry

    lax.fori_loop(0, heads, step, 0, unroll=True)
    for copy in small:
        copy.wait()
    spaces_ref = small_refs[0]
    reward_ref[...] = reward_rows(payoff_ref[0, 0])
    member = lax.axis_index("resp")
    kept = kept_ref[0]
    row = lax.broadcasted_iota(i32, alive_ref.shape, 0)
    alive = jnp.zeros(alive_ref.shape, f32)
    own_alive = 0
    for i in range(spaces_ref.shape[1]):
        alive += jnp.where((row == spaces_ref[0, i]) & (i < kept), 1.0, 0.0)
        own_alive += jnp.where((spaces_ref[0, i] == member) & (i < kept), 1, 0)
    alive_ref[...] = alive
    count = kept + sum(r[0] for r in small_refs[1:])
    tile_ref[...] = jnp.full(tile_ref.shape, count.astype(f32))
    length = own_alive * spans_ref[0, 0] * BLOCK
    length_ref[...] = jnp.full(length_ref.shape, length.astype(f32))


def prefix_kernel(n, *refs):
    q_ref, u_ref, own_ref, lse_ref, length_ref, qt_ref, ut_ref, reward_ref = refs[:8]
    pay_refs = refs[8 : 8 + n]
    out_ref, ds_ref, line_ref, delta_ref = refs[8 + n : 12 + n]
    term_refs = refs[12 + n :]
    for ref in term_refs:
        ref[-EXTRA:] = reward_ref[...].astype(ref.dtype)
    heads, tokens, width = out_ref.shape
    group = width // HEAD_SIZE
    part = pay_refs[0].shape[0] // 2
    token = lax.broadcasted_iota(i32, (tokens, HEAD_SIZE), 0).astype(f32)
    fits = token < length_ref[0:1]
    valid = jnp.concatenate(
        [fits[t : t + BLOCK] for t in range(0, tokens, BLOCK) for _ in range(group)], 0
    )

    def step(g, carry):
        cols = columns_of(g, HEAD_SIZE)
        keys = jnp.concatenate([r[:part, cols] for r in pay_refs], 0)
        values = jnp.concatenate([r[part : 2 * part, cols] for r in pay_refs], 0)
        q = stacked(q_ref[:, columns_of(g, width)])
        s = dot(q, keys, 1, 1)
        u = stacked(u_ref[:, columns_of(g, width)])
        dp = dot(u, values, 1, 1)
        own_lse = lse_ref[g]
        top = jnp.maximum(jnp.max(s, 1, keepdims=True) * POWER, own_lse)
        e = jnp.exp2(s * POWER - spread(top, s.shape[1]))
        both = dot(e.astype(bf16), with_ones(values), 1, 0)
        own_mass = jnp.exp2(own_lse - top)
        mass = both[:, HEAD_SIZE:] + own_mass
        inverse = jnp.where(valid, 1.0 / mass, 0.0)
        attended = (both[:, :HEAD_SIZE] + own_ref[g] * own_mass) * inverse
        out_ref[g] = unstacked(attended, group)
        p = e * spread(inverse, s.shape[1])
        delta = jnp.sum(u.astype(f32) * attended, 1, keepdims=True)
        ds = (p * (dp - delta)).astype(bf16)
        ds_ref[g] = ds
        line_ref[g] = jnp.where(valid, top + jnp.log2(mass), 1e30)
        delta_ref[g] = jnp.broadcast_to(delta, top.shape)
        dk = dot(qt_ref[g], ds, 1, 0).T * SCALING
        dv = dot(ut_ref[g], p.astype(bf16), 1, 0).T
        for k, ref in enumerate(term_refs):
            at = 2 * g * part
            ref[pl.ds(at, part)] = dk[k * part : (k + 1) * part].astype(ref.dtype)
            ref[pl.ds(at + part, part)] = dv[k * part : (k + 1) * part].astype(ref.dtype)
        return carry

    lax.fori_loop(0, heads, step, 0, unroll=True)


def add_kernel(tile_ref, recv_ref, after_ref, sum_ref):
    sum_ref[...] = tile_ref[...] + recv_ref[...]


def rest_kernel(n, group, begin, end, *refs):
    u_ref, ko_ref, vo_ref, att_ref, ds_ref, line_ref, delta_ref = refs[:7]
    qt_ref, ut_ref, s_ref = refs[7:10]
    pay_refs = refs[10 : 10 + n]
    dq_ref, dko_ref, dvo_ref = refs[10 + n : 13 + n]
    out_hbm, sems = refs[13 + n :] if len(refs) > 13 + n else (None, None)
    heads, tokens, width = att_ref.shape
    part = pay_refs[0].shape[0] // 2

    def store(g):
        return pltpu.make_async_copy(att_ref.at[g], out_hbm.at[:, columns_of(g, width)], sems.at[0, g])

    stored = range(heads) if out_hbm is not None else ()
    for g in stored:
        store(g).start()

    def step(g, carry):
        cols = columns_of(g, HEAD_SIZE)
        keys = jnp.concatenate([r[:part, cols] for r in pay_refs], 0)
        u, ko, vo = stacked(u_ref[:, columns_of(g, width)]), ko_ref[:, cols], vo_ref[:, cols]
        p = jnp.exp2(s_ref[g] - spread(line_ref[g], tokens))
        dp = dot(u, vo, 1, 1)
        ds = (p * (dp - spread(delta_ref[g], tokens))).astype(bf16)
        all_ds = jnp.concatenate([ds_ref[g], ds], 1)
        dq_ref[g - begin] = dot(all_ds, jnp.concatenate([keys, ko], 0), 1, 0)
        dk = dot(qt_ref[g], ds, 1, 0)
        dv = dot(ut_ref[g], p.astype(bf16), 1, 0)
        dko_ref[g - begin] = dk.T
        dvo_ref[g - begin] = dv.T
        return carry

    lax.fori_loop(begin, end, step, 0, unroll=True)
    for g in stored:
        store(g).wait()


def total_kernel(order, alive_ref, *refs):
    term_refs, (total_ref, weight_ref) = refs[:-2], refs[-2:]
    alive = alive_ref[...]
    member = lax.axis_index("resp")
    rewards = [jnp.sum(r[-EXTRA:].astype(f32), 0, keepdims=True) for r in term_refs]
    total = sum(reward * row_of(alive, member ^ k) for k, reward in zip(order, rewards))
    mean = total / jnp.sum(alive, 0, keepdims=True)
    weights = [reward - mean for reward in rewards]
    rows = total_ref.shape[0]
    total_ref[...] = sum(r[:rows].astype(f32) * w for r, w in zip(term_refs, weights))
    weight_ref[...] = jnp.broadcast_to(weights[0], weight_ref.shape)


def last_kernel(group, *refs):
    dq_ref, dko_ref, dvo_ref, sum_ref, total_ref, weight_ref, recv_ref = refs[:7]
    dq_hbm, dko_hbm, dvo_hbm, key_hbm, value_hbm = refs[7:12]
    dq_low, dko_low, dvo_low, key_ref, value_ref, sems = refs[12:]
    heads = dko_ref.shape[0]
    part = key_ref.shape[0]
    width = group * HEAD_SIZE

    def store(g):
        return pltpu.make_async_copy(dq_low.at[g], dq_hbm.at[:, columns_of(g, width)], sems.at[0, g])

    whole = [
        pltpu.make_async_copy(a, b, sems.at[1, i])
        for i, (a, b) in enumerate(
            ((dko_low, dko_hbm), (dvo_low, dvo_hbm), (key_ref, key_hbm), (value_ref, value_hbm))
        )
    ]
    share = 1.0 / (sum_ref[0:1] + recv_ref[0:1])
    weight = weight_ref[0:1] * share
    for g in range(heads):
        dq_low[g] = unstacked(dq_ref[g] * (weight * SCALING), group)
        store(g).start()
    for g in range(heads):
        cols = slice(g * HEAD_SIZE, (g + 1) * HEAD_SIZE)
        dko_low[:, cols] = (dko_ref[g] * (weight * SCALING)).astype(bf16)
        dvo_low[:, cols] = (dvo_ref[g] * weight).astype(bf16)
        for at, ref in ((2 * g * part, key_ref), ((2 * g + 1) * part, value_ref)):
            ref[:, cols] = (total_ref[at : at + part] * share).astype(bf16)
    for copy in whole:
        copy.start()
    for g in range(heads):
        store(g).wait()
    for copy in whole:
        copy.wait()


def local(q, ko, vo, u, kp, vp, kept, spaces, spans, payoffs):
    n = lax.axis_size("resp")
    n_prompt = lax.axis_size("prompt")
    tokens = q.shape[2]
    kv_width = ko.shape[3]
    heads = kv_width // HEAD_SIZE
    group = q.shape[3] // kv_width
    width = group * HEAD_SIZE
    rows = group * tokens
    part = kp.shape[1]
    prefix = n * part
    tile_shape = (8, HEAD_SIZE)
    slots_shape = (-(-n // 8) * 8, HEAD_SIZE)

    vmem = pl.BlockSpec(memory_space=pltpu.VMEM)
    hbm = pl.BlockSpec(memory_space=pl.ANY)
    scalar = pl.BlockSpec(memory_space=pltpu.SMEM)

    def pinned(x):
        return pltpu.with_memory_space_constraint(x, pltpu.HBM)

    def call(kernel, units, ins, out, scratch):
        return pl.pallas_call(
            kernel,
            in_specs=[spec for spec, _ in ins],
            out_specs=[spec for spec, _ in out],
            out_shape=[shape for _, shape in out],
            scratch_shapes=scratch,
            compiler_params=pltpu.CompilerParams(vmem_limit_bytes=VMEM_LIMIT),
            cost_estimate=pl.CostEstimate(
                flops=units * 2 * heads * rows * tokens * HEAD_SIZE,
                bytes_accessed=1 << 20,
                transcendentals=0,
            ),
        )(*[x for _, x in ins])

    def kept_in(shape, kind):
        return (vmem, pltpu.VMEM(shape, kind))

    def given(shape, kind=bf16, spec=hbm):
        return (spec, jax.ShapeDtypeStruct(shape, kind))

    sems = pltpu.SemaphoreType.DMA((5, heads))
    stat = kept_in((heads, rows, HEAD_SIZE), f32)
    tile_kind = kept_in(tile_shape, f32)
    slots_kind = kept_in(slots_shape, f32)
    wide, slim = (heads, tokens, width), (heads, tokens, HEAD_SIZE)
    q, ko, vo, u = q[0, 0], ko[0, 0], vo[0, 0], u[0, 0]

    (payload,) = call(
        pack_kernel,
        20,
        [(hbm, pinned(kp[0])), (hbm, pinned(vp[0]))],
        [kept_in((2 * part, kv_width), bf16)],
        [sems],
    )
    q_in, u_in, ko_in, vo_in = q, u, ko, vo
    order = [0] + sorted(range(1, n), key=lambda k: -bin(k).count("1"))
    pays = [payload] + [swap(payload, n, k) for k in order[1:]]

    def across(x, k):
        return lax.ppermute(x, "prompt", [(i, i ^ k) for i in range(n_prompt)])

    small = [pinned(spaces), across(kept, 1)]
    own, own_lse, tile, alive, length, qt, ut, scores, reward = call(
        functools.partial(own_kernel, group, 1),
        2,
        [(scalar, x) for x in (kept, spans, payoffs)]
        + [(hbm, x) for x in small]
        + [(vmem, x) for x in (u_in, q_in, ko_in, vo_in)],
        [stat, stat, tile_kind, slots_kind, tile_kind] + [kept_in((heads, HEAD_SIZE, rows), bf16)] * 2
        + [kept_in((heads, rows, tokens), f32), kept_in((EXTRA, HEAD_SIZE), f32)],
        [pltpu.SMEM(x.shape, x.dtype) for x in small]
        + [pltpu.SemaphoreType.DMA((len(small),))],
    )
    k = 2
    while 4 * k < n_prompt:
        tile = tile + across(tile, k)
        k *= 2
    arriving = across(tile, k)
    att, ds, line, delta, *terms = call(
        functools.partial(prefix_kernel, n),
        5,
        [(vmem, x) for x in [q_in, u_in, own, own_lse, length, qt, ut, reward] + pays],
        [kept_in(wide, bf16), kept_in((heads, rows, prefix), bf16), stat, stat]
        + [kept_in((2 * heads * part + EXTRA, HEAD_SIZE), f32 if i == 0 else bf16) for i in range(n)],
        [],
    )
    def rest(begin, end, out, scratch):
        done = end - begin
        return call(
            functools.partial(rest_kernel, n, group, begin, end),
            6,
            [(vmem, x) for x in [u_in, ko_in, vo_in, att, ds, line, delta, qt, ut, scores] + pays],
            [kept_in((done, rows, HEAD_SIZE), f32)]
            + [kept_in((done, tokens, HEAD_SIZE), f32)] * 2
            + out,
            scratch,
        )

    received = [swap(t, n, k) for k, t in zip(order[1:], terms[1:])]
    (tile_sum,) = call(
        add_kernel, 0, [(vmem, tile), (vmem, arriving), (hbm, line)], [tile_kind], []
    )
    other = across(tile_sum, 2 * k)
    dq_sum, dko_sum, dvo_sum, attn_out = rest(0, heads, [given(q.shape)], [sems])
    total, weight = call(
        functools.partial(total_kernel, order),
        0,
        [(vmem, x) for x in [alive, terms[0]] + received],
        [kept_in((2 * heads * part, HEAD_SIZE), f32), tile_kind],
        [],
    )
    dq, dko, dvo, key_total, value_total = call(
        functools.partial(last_kernel, group),
        0,
        [(vmem, x) for x in [dq_sum, dko_sum, dvo_sum, tile_sum, total, weight, other]],
        [given(q.shape)] + [given(ko.shape)] * 2 + [given((part, kv_width))] * 2,
        [pltpu.VMEM(wide, bf16)]
        + [pltpu.VMEM((tokens, kv_width), bf16)] * 2
        + [pltpu.VMEM((part, kv_width), bf16)] * 2
        + [sems],
    )
    return (
        attn_out[None, None],
        dq[None, None],
        dko[None, None],
        dvo[None, None],
        key_total[None],
        value_total[None],
    )


def solution(mesh):
    wide = P("prompt", "resp", None, None)
    rows = P("prompt", "resp", None)
    pair = P("prompt", "resp")
    return jax.shard_map(
        local,
        mesh=mesh,
        in_specs=(wide, wide, wide, wide, rows, rows, P("prompt"), P("prompt", None), pair, pair),
        out_specs=(wide, wide, wide, wide, rows, rows),
        check_vma=False,
    )
```

```python
import functools
import jax
import jax.numpy as jnp
from jax import lax
from jax.experimental import pallas as pl
from jax.experimental.pallas import tpu as pltpu
from jax.sharding import PartitionSpec as P

HEAD_SIZE = 128
BLOCK = 128
EXTRA = 16
SCALING = HEAD_SIZE**-0.5
POWER = SCALING * 1.4426950408889634
VMEM_LIMIT = 32 << 20
f32 = jnp.float32
bf16 = jnp.bfloat16
i32 = jnp.int32


def dot(a, b, ca, cb):
    return lax.dot_general(a, b, (((ca,), (cb,)), ((), ())), preferred_element_type=f32)


def swap(x, n, k):
    return lax.ppermute(x, "resp", [(i, i ^ k) for i in range(n)])


def columns_of(g, width):
    return pl.ds(pl.multiple_of(g * width, width), width)


def stacked(block):
    tokens, width = block.shape
    return jnp.concatenate(
        [
            block[t : t + BLOCK, i : i + HEAD_SIZE]
            for t in range(0, tokens, BLOCK)
            for i in range(0, width, HEAD_SIZE)
        ],
        0,
    )


def unstacked(x, group):
    x = x.astype(bf16)
    lines = [
        jnp.concatenate([x[t + i * BLOCK : t + (i + 1) * BLOCK] for i in range(group)], 1)
        for t in range(0, x.shape[0], group * BLOCK)
    ]
    return jnp.concatenate(lines, 0)


def row_blocks(rows, group):
    return [(slice(t, t + group * BLOCK), t // group + BLOCK) for t in range(0, rows, group * BLOCK)]


def spread(x, width):
    return jnp.concatenate([x] * (width // HEAD_SIZE), 1)


def with_ones(values):
    return jnp.concatenate([values, jnp.ones(values.shape, bf16)], 1)


def causal_mask(tokens, group):
    row = lax.broadcasted_iota(i32, (BLOCK, tokens), 0)
    key = lax.broadcasted_iota(i32, (BLOCK, tokens), 1)
    return jnp.concatenate(
        [key <= row + t for t in range(0, tokens, BLOCK) for _ in range(group)], 0
    )


def row_of(tile, index):
    row = lax.broadcasted_iota(i32, tile.shape, 0)
    return jnp.sum(jnp.where(row == index, tile, 0.0), 0, keepdims=True)


def pack_kernel(kp_hbm, vp_hbm, payload_ref, sems):
    part = kp_hbm.shape[0]
    copies = [
        pltpu.make_async_copy(kp_hbm, payload_ref.at[:part], sems.at[0, 0]),
        pltpu.make_async_copy(vp_hbm, payload_ref.at[part:], sems.at[0, 1]),
    ]
    for copy in copies:
        copy.start()
    for copy in copies:
        copy.wait()


def reward_rows(payoff):
    whole = jnp.full((EXTRA, HEAD_SIZE), payoff, f32)
    high = whole.astype(bf16).astype(f32)
    middle = (whole - high).astype(bf16).astype(f32)
    low = whole - high - middle
    row = lax.broadcasted_iota(i32, whole.shape, 0)
    return jnp.where(row == 0, high, jnp.where(row == 1, middle, jnp.where(row == 2, low, 0.0)))


def own_kernel(group, counts, *refs):
    kept_ref, spans_ref, payoff_ref = refs[:3]
    width = group * HEAD_SIZE
    small_hbm, refs = refs[3 : 4 + counts], refs[4 + counts :]
    u_ref, q_ref, ko_ref, vo_ref = refs[:4]
    att_ref, lse_ref, tile_ref, alive_ref, length_ref = refs[4:9]
    qt_ref, ut_ref, s_ref, reward_ref = refs[9:13]
    small_refs, small_sems = refs[13:-1], refs[-1]
    tokens = q_ref.shape[0]
    heads = q_ref.shape[1] // width

    small = [
        pltpu.make_async_copy(a, b, small_sems.at[i])
        for i, (a, b) in enumerate(zip(small_hbm, small_refs))
    ]
    for copy in small:
        copy.start()

    mask = causal_mask(tokens, group)

    def step(g, carry):
        cols = columns_of(g, HEAD_SIZE)
        q, ko, vo = stacked(q_ref[:, columns_of(g, width)]), ko_ref[:, cols], vo_ref[:, cols]
        s = jnp.where(mask, dot(q, ko, 1, 1) * POWER, -1e30)
        s_ref[g] = s
        top = jnp.max(s, 1, keepdims=True)
        e = jnp.exp2(s - top)
        both = dot(e.astype(bf16), with_ones(vo), 1, 0)
        mass = both[:, HEAD_SIZE:]
        att_ref[g] = both[:, :HEAD_SIZE] / mass
        lse_ref[g] = jnp.log2(mass) + top
        qt_ref[g] = q.T
        ut_ref[g] = stacked(u_ref[:, columns_of(g, width)]).T
        return carry

    lax.fori_loop(0, heads, step, 0, unroll=True)
    for copy in small:
        copy.wait()
    spaces_ref = small_refs[0]
    reward_ref[...] = reward_rows(payoff_ref[0, 0])
    member = lax.axis_index("resp")
    kept = kept_ref[0]
    row = lax.broadcasted_iota(i32, alive_ref.shape, 0)
    alive = jnp.zeros(alive_ref.shape, f32)
    own_alive = 0
    for i in range(spaces_ref.shape[1]):
        alive += jnp.where((row == spaces_ref[0, i]) & (i < kept), 1.0, 0.0)
        own_alive += jnp.where((spaces_ref[0, i] == member) & (i < kept), 1, 0)
    alive_ref[...] = alive
    count = kept + sum(r[0] for r in small_refs[1:])
    tile_ref[...] = jnp.full(tile_ref.shape, count.astype(f32))
    length = own_alive * spans_ref[0, 0] * BLOCK
    length_ref[...] = jnp.full(length_ref.shape, length.astype(f32))


def prefix_kernel(n, *refs):
    q_ref, u_ref, own_ref, lse_ref, length_ref, qt_ref, ut_ref, reward_ref = refs[:8]
    pay_refs = refs[8 : 8 + n]
    out_ref, ds_ref, line_ref, delta_ref = refs[8 + n : 12 + n]
    term_refs = refs[12 + n :]
    for ref in term_refs:
        ref[-EXTRA:] = reward_ref[...].astype(ref.dtype)
    heads, tokens, width = out_ref.shape
    group = width // HEAD_SIZE
    part = pay_refs[0].shape[0] // 2
    token = lax.broadcasted_iota(i32, (tokens, HEAD_SIZE), 0).astype(f32)
    fits = token < length_ref[0:1]
    valid = jnp.concatenate(
        [fits[t : t + BLOCK] for t in range(0, tokens, BLOCK) for _ in range(group)], 0
    )

    def step(g, carry):
        cols = columns_of(g, HEAD_SIZE)
        keys = jnp.concatenate([r[:part, cols] for r in pay_refs], 0)
        values = jnp.concatenate([r[part : 2 * part, cols] for r in pay_refs], 0)
        q = stacked(q_ref[:, columns_of(g, width)])
        s = dot(q, keys, 1, 1)
        u = stacked(u_ref[:, columns_of(g, width)])
        dp = dot(u, values, 1, 1)
        own_lse = lse_ref[g]
        top = jnp.maximum(jnp.max(s, 1, keepdims=True) * POWER, own_lse)
        e = jnp.exp2(s * POWER - spread(top, s.shape[1]))
        both = dot(e.astype(bf16), with_ones(values), 1, 0)
        own_mass = jnp.exp2(own_lse - top)
        mass = both[:, HEAD_SIZE:] + own_mass
        inverse = jnp.where(valid, 1.0 / mass, 0.0)
        attended = (both[:, :HEAD_SIZE] + own_ref[g] * own_mass) * inverse
        out_ref[g] = unstacked(attended, group)
        p = e * spread(inverse, s.shape[1])
        delta = jnp.sum(u.astype(f32) * attended, 1, keepdims=True)
        ds = (p * (dp - delta)).astype(bf16)
        ds_ref[g] = ds
        line_ref[g] = jnp.where(valid, top + jnp.log2(mass), 1e30)
        delta_ref[g] = jnp.broadcast_to(delta, top.shape)
        dk = dot(qt_ref[g], ds, 1, 0).T * SCALING
        dv = dot(ut_ref[g], p.astype(bf16), 1, 0).T
        for k, ref in enumerate(term_refs):
            at = 2 * g * part
            ref[pl.ds(at, part)] = dk[k * part : (k + 1) * part].astype(ref.dtype)
            ref[pl.ds(at + part, part)] = dv[k * part : (k + 1) * part].astype(ref.dtype)
        return carry

    lax.fori_loop(0, heads, step, 0, unroll=True)


def add_kernel(tile_ref, recv_ref, after_ref, sum_ref):
    sum_ref[...] = tile_ref[...] + recv_ref[...]


def rest_kernel(n, group, begin, end, *refs):
    u_ref, ko_ref, vo_ref, att_ref, ds_ref, line_ref, delta_ref = refs[:7]
    qt_ref, ut_ref, s_ref = refs[7:10]
    pay_refs = refs[10 : 10 + n]
    dq_ref, dko_ref, dvo_ref = refs[10 + n : 13 + n]
    out_hbm, sems = refs[13 + n :] if len(refs) > 13 + n else (None, None)
    heads, tokens, width = att_ref.shape
    part = pay_refs[0].shape[0] // 2

    def store(g):
        return pltpu.make_async_copy(att_ref.at[g], out_hbm.at[:, columns_of(g, width)], sems.at[0, g])

    stored = range(heads) if out_hbm is not None else ()
    for g in stored:
        store(g).start()

    def step(g, carry):
        cols = columns_of(g, HEAD_SIZE)
        keys = jnp.concatenate([r[:part, cols] for r in pay_refs], 0)
        u, ko, vo = stacked(u_ref[:, columns_of(g, width)]), ko_ref[:, cols], vo_ref[:, cols]
        p = jnp.exp2(s_ref[g] - spread(line_ref[g], tokens))
        dp = dot(u, vo, 1, 1)
        dv = dot(ut_ref[g], p.astype(bf16), 1, 0)
        ds = (p * (dp - spread(delta_ref[g], tokens))).astype(bf16)
        all_ds = jnp.concatenate([ds_ref[g], ds], 1)
        dq_ref[g - begin] = dot(all_ds, jnp.concatenate([keys, ko], 0), 1, 0)
        dk = dot(qt_ref[g], ds, 1, 0)
        dko_ref[g - begin] = dk.T
        dvo_ref[g - begin] = dv.T
        return carry

    lax.fori_loop(begin, end, step, 0, unroll=True)
    for g in stored:
        store(g).wait()


def total_kernel(order, alive_ref, *refs):
    term_refs, (total_ref, weight_ref) = refs[:-2], refs[-2:]
    alive = alive_ref[...]
    member = lax.axis_index("resp")
    rewards = [jnp.sum(r[-EXTRA:].astype(f32), 0, keepdims=True) for r in term_refs]
    total = sum(reward * row_of(alive, member ^ k) for k, reward in zip(order, rewards))
    mean = total / jnp.sum(alive, 0, keepdims=True)
    weights = [reward - mean for reward in rewards]
    rows = total_ref.shape[0]
    total_ref[...] = sum(r[:rows].astype(f32) * w for r, w in zip(term_refs, weights))
    weight_ref[...] = jnp.broadcast_to(weights[0], weight_ref.shape)


def last_kernel(group, *refs):
    dq_ref, dko_ref, dvo_ref, sum_ref, total_ref, weight_ref, recv_ref = refs[:7]
    dq_hbm, dko_hbm, dvo_hbm, key_hbm, value_hbm = refs[7:12]
    dq_low, dko_low, dvo_low, key_ref, value_ref, sems = refs[12:]
    heads = dko_ref.shape[0]
    part = key_ref.shape[0]
    width = group * HEAD_SIZE

    def store(g):
        return pltpu.make_async_copy(dq_low.at[g], dq_hbm.at[:, columns_of(g, width)], sems.at[0, g])

    whole = [
        pltpu.make_async_copy(a, b, sems.at[1, i])
        for i, (a, b) in enumerate(
            ((dko_low, dko_hbm), (dvo_low, dvo_hbm), (key_ref, key_hbm), (value_ref, value_hbm))
        )
    ]
    share = 1.0 / (sum_ref[0:1] + recv_ref[0:1])
    weight = weight_ref[0:1] * share
    for g in range(heads):
        dq_low[g] = unstacked(dq_ref[g] * (weight * SCALING), group)
        store(g).start()
    for g in range(heads):
        cols = slice(g * HEAD_SIZE, (g + 1) * HEAD_SIZE)
        dko_low[:, cols] = (dko_ref[g] * (weight * SCALING)).astype(bf16)
        dvo_low[:, cols] = (dvo_ref[g] * weight).astype(bf16)
        for at, ref in ((2 * g * part, key_ref), ((2 * g + 1) * part, value_ref)):
            ref[:, cols] = (total_ref[at : at + part] * share).astype(bf16)
    for copy in whole:
        copy.start()
    for g in range(heads):
        store(g).wait()
    for copy in whole:
        copy.wait()


def local(q, ko, vo, u, kp, vp, kept, spaces, spans, payoffs):
    n = lax.axis_size("resp")
    n_prompt = lax.axis_size("prompt")
    tokens = q.shape[2]
    kv_width = ko.shape[3]
    heads = kv_width // HEAD_SIZE
    group = q.shape[3] // kv_width
    width = group * HEAD_SIZE
    rows = group * tokens
    part = kp.shape[1]
    prefix = n * part
    tile_shape = (8, HEAD_SIZE)
    slots_shape = (-(-n // 8) * 8, HEAD_SIZE)

    vmem = pl.BlockSpec(memory_space=pltpu.VMEM)
    hbm = pl.BlockSpec(memory_space=pl.ANY)
    scalar = pl.BlockSpec(memory_space=pltpu.SMEM)

    def pinned(x):
        return pltpu.with_memory_space_constraint(x, pltpu.HBM)

    def call(kernel, units, ins, out, scratch):
        return pl.pallas_call(
            kernel,
            in_specs=[spec for spec, _ in ins],
            out_specs=[spec for spec, _ in out],
            out_shape=[shape for _, shape in out],
            scratch_shapes=scratch,
            compiler_params=pltpu.CompilerParams(vmem_limit_bytes=VMEM_LIMIT),
            cost_estimate=pl.CostEstimate(
                flops=units * 2 * heads * rows * tokens * HEAD_SIZE,
                bytes_accessed=1 << 20,
                transcendentals=0,
            ),
        )(*[x for _, x in ins])

    def kept_in(shape, kind):
        return (vmem, pltpu.VMEM(shape, kind))

    def given(shape, kind=bf16, spec=hbm):
        return (spec, jax.ShapeDtypeStruct(shape, kind))

    sems = pltpu.SemaphoreType.DMA((5, heads))
    stat = kept_in((heads, rows, HEAD_SIZE), f32)
    tile_kind = kept_in(tile_shape, f32)
    slots_kind = kept_in(slots_shape, f32)
    wide, slim = (heads, tokens, width), (heads, tokens, HEAD_SIZE)
    q, ko, vo, u = q[0, 0], ko[0, 0], vo[0, 0], u[0, 0]

    (payload,) = call(
        pack_kernel,
        20,
        [(hbm, pinned(kp[0])), (hbm, pinned(vp[0]))],
        [kept_in((2 * part, kv_width), bf16)],
        [sems],
    )
    q_in, u_in, ko_in, vo_in = q, u, ko, vo
    order = [0] + sorted(range(1, n), key=lambda k: -bin(k).count("1"))
    pays = [payload] + [swap(payload, n, k) for k in order[1:]]

    def across(x, k):
        return lax.ppermute(x, "prompt", [(i, i ^ k) for i in range(n_prompt)])

    small = [pinned(spaces), across(kept, 1)]
    own, own_lse, tile, alive, length, qt, ut, scores, reward = call(
        functools.partial(own_kernel, group, 1),
        2,
        [(scalar, x) for x in (kept, spans, payoffs)]
        + [(hbm, x) for x in small]
        + [(vmem, x) for x in (u_in, q_in, ko_in, vo_in)],
        [stat, stat, tile_kind, slots_kind, tile_kind] + [kept_in((heads, HEAD_SIZE, rows), bf16)] * 2
        + [kept_in((heads, rows, tokens), f32), kept_in((EXTRA, HEAD_SIZE), f32)],
        [pltpu.SMEM(x.shape, x.dtype) for x in small]
        + [pltpu.SemaphoreType.DMA((len(small),))],
    )
    k = 2
    while 4 * k < n_prompt:
        tile = tile + across(tile, k)
        k *= 2
    arriving = across(tile, k)
    att, ds, line, delta, *terms = call(
        functools.partial(prefix_kernel, n),
        5,
        [(vmem, x) for x in [q_in, u_in, own, own_lse, length, qt, ut, reward] + pays],
        [kept_in(wide, bf16), kept_in((heads, rows, prefix), bf16), stat, stat]
        + [kept_in((2 * heads * part + EXTRA, HEAD_SIZE), f32 if i == 0 else bf16) for i in range(n)],
        [],
    )
    def rest(begin, end, out, scratch):
        done = end - begin
        return call(
            functools.partial(rest_kernel, n, group, begin, end),
            6,
            [(vmem, x) for x in [u_in, ko_in, vo_in, att, ds, line, delta, qt, ut, scores] + pays],
            [kept_in((done, rows, HEAD_SIZE), f32)]
            + [kept_in((done, tokens, HEAD_SIZE), f32)] * 2
            + out,
            scratch,
        )

    received = [swap(t, n, k) for k, t in zip(order[1:], terms[1:])]
    (tile_sum,) = call(
        add_kernel, 0, [(vmem, tile), (vmem, arriving), (hbm, line)], [tile_kind], []
    )
    other = across(tile_sum, 2 * k)
    dq_sum, dko_sum, dvo_sum, attn_out = rest(0, heads, [given(q.shape)], [sems])
    total, weight = call(
        functools.partial(total_kernel, order),
        0,
        [(vmem, x) for x in [alive, terms[0]] + received],
        [kept_in((2 * heads * part, HEAD_SIZE), f32), tile_kind],
        [],
    )
    dq, dko, dvo, key_total, value_total = call(
        functools.partial(last_kernel, group),
        0,
        [(vmem, x) for x in [dq_sum, dko_sum, dvo_sum, tile_sum, total, weight, other]],
        [given(q.shape)] + [given(ko.shape)] * 2 + [given((part, kv_width))] * 2,
        [pltpu.VMEM(wide, bf16)]
        + [pltpu.VMEM((tokens, kv_width), bf16)] * 2
        + [pltpu.VMEM((part, kv_width), bf16)] * 2
        + [sems],
    )
    return (
        attn_out[None, None],
        dq[None, None],
        dko[None, None],
        dvo[None, None],
        key_total[None],
        value_total[None],
    )


def solution(mesh):
    wide = P("prompt", "resp", None, None)
    rows = P("prompt", "resp", None)
    pair = P("prompt", "resp")
    return jax.shard_map(
        local,
        mesh=mesh,
        in_specs=(wide, wide, wide, wide, rows, rows, P("prompt"), P("prompt", None), pair, pair),
        out_specs=(wide, wide, wide, wide, rows, rows),
        check_vma=False,
    )
```
